512 devices in a mesh: grp: 16 (over x, y_lo), cell: 32 (over z, y_hi, core).
Axes of the slice: x: 4, y: 8 (y_hi: 2, y_lo: 4; y = y_hi * 4 + y_lo), z: 8, core: 2. Of those that a mesh axis runs over, the one named last changes fastest.
Arguments:
- snapshots: bfloat16 [98304, 2048], P('cell', 'grp'), may hold values from -40 to 40
- density: float32 [8], replicated, may hold values from 0.25 to 4
Outputs:
- gram: float32 [2048, 2048], P('grp', 'cell')
The draws below stay inside these ranges and needn't reach their ends.
All inputs are finite; a program needn't handle non-finite values.
Results may differ from the reference program's by a relative error of at most 0.00074.
Values may be sent and summed in bfloat16 or wider, within the bound.
A program may use at most 64 MiB of HBM per device.

```python
import math
import jax
import jax.numpy as jnp
from jax import lax

REG = 8
NS = 2048
NC = 98304
N_CELL = 32


def draw_snapshots(key, part):
    key = jax.random.fold_in(key, 11)
    noise_key, cell_key, snap_key = jax.random.split(key, 3)
    cell_scale = jnp.exp(jax.random.uniform(cell_key, (NC,), jnp.float32, -1.15, 1.15))
    snap_scale = jnp.exp(jax.random.uniform(snap_key, (NS,), jnp.float32, -1.15, 1.15))
    fields = jnp.clip(jax.random.normal(noise_key, (NC, NS), jnp.float32), -4.0, 4.0)
    return (fields * cell_scale[:, None] * snap_scale[None, :]).astype(jnp.bfloat16)


def setup_inputs(seed: int = 0) -> dict:
    seeds = jax.random.split(jax.random.key(seed), 3)
    return {
        "snapshots": draw_snapshots(jax.random.fold_in(seeds[2], 71), 0),
        "density": jnp.clip(jnp.exp(jax.random.uniform(seeds[1], (REG,), jnp.float32, math.log(0.25), math.log(4.0))), 0.25, 4.0),
    }


def reference(snapshots, density):
    total_cells = snapshots.shape[0]
    positions = jnp.arange(total_cells, dtype=jnp.int32)
    zones = positions * REG // total_cells
    scales = jnp.sqrt(density)[zones]
    weighted = (snapshots.astype(jnp.float32) * scales[:, None]).astype(jnp.bfloat16)
    blocks = weighted.reshape(N_CELL, total_cells // N_CELL, weighted.shape[1])

    def accumulate(total, block):
        wide = block.astype(jnp.float32)
        return (total + jnp.dot(wide.T, wide, precision=lax.Precision.HIGHEST), None)
    start = jnp.zeros((weighted.shape[1], weighted.shape[1]), jnp.float32)
    total, unused = lax.scan(accumulate, start, blocks)
    return total / total_cells
```

```python
import jax
import jax.numpy as jnp
from jax import lax
from jax.experimental import pallas as pl
from jax.experimental.pallas import tpu as pltpu
from jax.sharding import PartitionSpec as P

MESH = pl.DeviceIdType.MESH
CELLS = 98304
SLAB = 3072
QUARTER = SLAB // 4
HALF = QUARTER // 2
SNAP = 128


def device(x, y, z, core):
    return x * 4 + y % 4, (z * 2 + y // 4) * 2 + core


def copy_to(src, dst, send, recv, target):
    return pltpu.make_async_remote_copy(
        src_ref=src, dst_ref=dst, send_sem=send, recv_sem=recv, device_id=target, device_id_type=MESH
    )


def kernel(
    snap_hbm, density_ref, out_ref,
    snap, turned, own, next1, next2, part, peer_part, arrived, total, tiles, mine, other,
    load_sem, y_send, y_recv, x1_send, x1_recv, x2_send, x2_recv, core_send, core_recv,
    ring_send, ring_recv, tile_send, tile_recv, last_send, last_recv, plane_sem, all_sem,
):
    grp, cell = lax.axis_index("grp"), lax.axis_index("cell")
    x, ylo, z, core = grp // 4, grp % 4, cell // 4, cell % 2
    y = (cell // 2) % 2 * 4 + ylo
    y_base = y - ylo
    peer = (grp, cell + 1 - 2 * core)

    load = pltpu.make_async_copy(snap_hbm, snap, load_sem)
    load.start()

    barrier = pltpu.get_barrier_semaphore()

    def greet(sem, d, axis):
        target = {
            "x": lambda: device((x + d) % 4, y, z, core),
            "y": lambda: device(x, (y + d) % 8, z, core),
            "z": lambda: device(x, y, (z + d) % 8, core),
        }[axis]()
        pl.semaphore_signal(sem, inc=1, device_id=target, device_id_type=MESH)

    for d in range(1, 4):
        greet(barrier, d, "x")
    for d in range(1, 8):
        greet(barrier, d, "y")
        greet(barrier, d, "z")
    pl.semaphore_signal(barrier, inc=1, device_id=peer, device_id_type=MESH)

    load.wait()
    scale = jnp.sqrt(jnp.full((1, SNAP), density_ref[z], jnp.float32))
    for q in range(4):
        block = snap[pl.ds(q * QUARTER, QUARTER), :].astype(jnp.float32) * scale
        turned[q] = block.astype(jnp.bfloat16).T
    own[ylo] = turned[ylo]
    pl.semaphore_wait(barrier, 18)

    def y_copy(q):
        return copy_to(
            turned.at[q], own.at[ylo], y_send.at[q], y_recv.at[ylo], device(x, y_base + q, z, core)
        )

    def y_arrival(q):
        return copy_to(turned.at[q], own.at[q], y_send.at[q], y_recv.at[q], device(x, y_base + q, z, core))

    def other_y(d):
        return (ylo + d) % 4

    for d in (1, 2, 3):
        y_copy(other_y(d)).start()

    half = x // 2
    half_next2 = ((x + 2) % 4) // 2

    def x1_copy(q):
        return copy_to(
            own.at[q], next1.at[q], x1_send.at[q], x1_recv.at[q], device((x + 3) % 4, y, z, core)
        )

    def x2_copy(q):
        lanes = pl.ds(pl.multiple_of(half_next2 * HALF, HALF), HALF)
        return copy_to(
            own.at[q, :, lanes], next2.at[q], x2_send.at[q], x2_recv.at[q], device((x + 2) % 4, y, z, core)
        )

    x1_copy(ylo).start()
    x2_copy(ylo).start()

    for d in range(1, 8):
        greet(plane_sem, d, "y")

    for d in (1, 2, 3):
        q = other_y(d)
        y_arrival(q).wait_recv()
        x1_copy(q).start()
        x2_copy(q).start()

    pl.semaphore_wait(plane_sem, 7)
    for d in range(1, 4):
        greet(all_sem, d, "x")

    def multiply(g, left, right):
        product = lax.dot_general(
            left, right, (((1,), (1,)), ((), ())), preferred_element_type=jnp.float32
        )
        for n in range(8):
            for h in range(2):
                for t in range(4):
                    part[g, h, t // 2, n, t % 2] = product[
                        n * 64 + h * 32 : n * 64 + h * 32 + 32, t * 128 : t * 128 + 128
                    ]

    def core_copy(g):
        return copy_to(part.at[g, 1 - core], peer_part.at[g], core_send.at[g], core_recv.at[g], peer)

    def ring_copy(g, colour, d):
        if colour == 0:
            here, there = z, (z + d) % 8
            target = device(x, y, there, core)
        else:
            here, there = y, (y + d) % 8
            target = device(x, there, z, core)
        return copy_to(
            part.at[g, core, colour, there],
            arrived.at[g, colour, here],
            ring_send.at[g, colour],
            ring_recv.at[g, colour],
            target,
        )

    def spread(g):
        core_copy(g).wait_recv()
        part[g, core] = part[g, core] + peer_part[g]

        @pl.loop(1, 8)
        def _(d):
            ring_copy(g, 0, d).start()
            ring_copy(g, 1, d).start()

    left = own[...].reshape(512, QUARTER)
    multiply(0, left, left)
    core_copy(0).start()

    for q in range(4):
        x1_copy(q).wait_recv()
    multiply(1, own[...].reshape(512, QUARTER), next1[...].reshape(512, QUARTER))
    core_copy(1).start()
    spread(0)

    for q in range(4):
        x2_copy(q).wait_recv()
    lanes = pl.ds(pl.multiple_of(half * HALF, HALF), HALF)
    multiply(2, own[:, :, lanes].reshape(512, HALF), next2[...].reshape(512, HALF))
    core_copy(2).start()
    spread(1)
    spread(2)
    pl.semaphore_wait(all_sem, 3)

    def tile_copies(g, colour, t, act):
        k = 2 * colour + t
        where, index = (z, y) if colour == 0 else (y, z)
        row = x * 4 + where // 2
        column = ((x + g) % 4) * 4 + k
        targets = [(0, row, 2 * column + core)]
        if g > 0:
            targets.append((1, column, 2 * row + core))
        for kind, to_grp, to_cell in targets:
            here = jnp.logical_and(to_grp == grp, to_cell == cell)
            src = total.at[g, colour, t]
            dst = tiles.at[kind, index, where % 2]
            act(src, dst, kind, here, (to_grp, to_cell))

    def start_tile(src, dst, kind, here, target):
        @pl.when(here)
        def _():
            pltpu.make_async_copy(src, dst, tile_recv.at[kind]).start()

        @pl.when(jnp.logical_not(here))
        def _():
            copy_to(src, dst, tile_send, tile_recv.at[kind], target).start()

    def finish_tile(src, dst, kind, here, target):
        @pl.when(jnp.logical_not(here))
        def _():
            copy_to(src, dst, tile_send, tile_recv.at[kind], target).wait_send()

    for g in range(3):
        for colour in range(2):
            here = z if colour == 0 else y
            seven = arrived.at[g, colour, pl.ds(0, 7)]
            copy_to(seven, seven, ring_send.at[g, colour], ring_recv.at[g, colour], peer).wait_recv()
            acc = part[g, core, colour, here]
            for d in range(1, 8):
                acc = acc + arrived[g, colour, (here + d) % 8]
            total[g, colour] = acc
            for t in range(2):
                tile_copies(g, colour, t, start_tile)

    apart = (cell // 8 - x) % 4
    for kind in range(2):
        used = apart != 3 if kind == 0 else apart >= 2

        @pl.when(used)
        def _(kind=kind):
            whole = tiles.at[kind]
            copy_to(whole, whole, tile_send, tile_recv.at[kind], peer).wait_recv()
            mine[kind] = jnp.sum(tiles[kind], axis=0)

        @pl.when(jnp.logical_not(used))
        def _(kind=kind):
            mine[kind] = jnp.zeros_like(mine[kind])

    last = copy_to(mine, other, last_send, last_recv, peer)
    last.start()

    for q in (1, 2, 3):
        y_copy(other_y(q)).wait_send()
    for q in range(4):
        x1_copy(q).wait_send()
        x2_copy(q).wait_send()
    for g in range(3):
        core_copy(g).wait_send()
        for colour in range(2):
            seven = arrived.at[g, colour, pl.ds(0, 7)]
            copy_to(seven, seven, ring_send.at[g, colour], ring_recv.at[g, colour], peer).wait_send()
            for t in range(2):
                tile_copies(g, colour, t, finish_tile)

    last.wait()
    first = core == 0
    low = jnp.where(first, mine[...], other[...])
    high = jnp.where(first, other[...], mine[...])

    def whole_tile(kind):
        return jnp.concatenate([low[kind, 0], high[kind, 0], low[kind, 1], high[kind, 1]], axis=0)

    full = (whole_tile(0) + whole_tile(1).T) * (1.0 / CELLS)
    out_ref[...] = jnp.where(first, full[:, :64], full[:, 64:])


def body(snapshots, density):
    f32, bf16, dma = jnp.float32, jnp.bfloat16, pltpu.SemaphoreType.DMA
    return pl.pallas_call(
        kernel,
        out_shape=jax.ShapeDtypeStruct((128, 64), f32),
        in_specs=[pl.BlockSpec(memory_space=pl.ANY), pl.BlockSpec(memory_space=pltpu.SMEM)],
        out_specs=pl.BlockSpec(memory_space=pltpu.VMEM),
        scratch_shapes=[
            pltpu.VMEM((SLAB, SNAP), bf16),
            pltpu.VMEM((4, SNAP, QUARTER), bf16),
            pltpu.VMEM((4, SNAP, QUARTER), bf16),
            pltpu.VMEM((4, SNAP, QUARTER), bf16),
            pltpu.VMEM((4, SNAP, HALF), bf16),
            pltpu.VMEM((3, 2, 2, 8, 2, 32, 128), f32),
            pltpu.VMEM((3, 2, 8, 2, 32, 128), f32),
            pltpu.VMEM((3, 2, 8, 2, 32, 128), f32),
            pltpu.VMEM((3, 2, 2, 32, 128), f32),
            pltpu.VMEM((2, 8, 2, 32, 128), f32),
            pltpu.VMEM((2, 2, 32, 128), f32),
            pltpu.VMEM((2, 2, 32, 128), f32),
            dma, dma((4,)), dma((4,)), dma((4,)), dma((4,)), dma((4,)), dma((4,)), dma((3,)), dma((3,)),
            dma((3, 2)), dma((3, 2)), dma, dma((2,)), dma, dma,
            pltpu.SemaphoreType.REGULAR, pltpu.SemaphoreType.REGULAR,
        ],
        compiler_params=pltpu.CompilerParams(
            collective_id=0, has_side_effects=True, vmem_limit_bytes=40 * 2**20
        ),
        cost_estimate=pl.CostEstimate(flops=10**9, bytes_accessed=10**6, transcendentals=0),
    )(snapshots, density)


def solution(mesh):
    in_specs = (P("cell", "grp"), P())
    return jax.shard_map(body, mesh=mesh, in_specs=in_specs, out_specs=P("grp", "cell"), check_vma=False)
```

```python
import jax
import jax.numpy as jnp
from jax import lax
from jax.experimental import pallas as pl
from jax.experimental.pallas import tpu as pltpu
from jax.sharding import PartitionSpec as P

MESH = pl.DeviceIdType.MESH
CELLS = 98304
SLAB = 3072
QUARTER = SLAB // 4
HALF = QUARTER // 2
SNAP = 128


def device(x, y, z, core):
    return x * 4 + y % 4, (z * 2 + y // 4) * 2 + core


def copy_to(src, dst, send, recv, target):
    return pltpu.make_async_remote_copy(
        src_ref=src, dst_ref=dst, send_sem=send, recv_sem=recv, device_id=target, device_id_type=MESH
    )


def kernel(
    snap_hbm, density_ref, out_ref,
    snap, turned, own, next1, next2, part, peer_part, arrived, total, crossed, piece, mine, other,
    load_sem, y_send, y_recv, x1_send, x1_recv, x2_send, x2_recv, core_send, core_recv,
    ring_send, ring_recv, cross_send, cross_recv, tile_send, tile_recv, last_send, last_recv, plane_sem, all_sem,
):
    grp, cell = lax.axis_index("grp"), lax.axis_index("cell")
    x, ylo, z, core = grp // 4, grp % 4, cell // 4, cell % 2
    y = (cell // 2) % 2 * 4 + ylo
    y_base = y - ylo
    peer = (grp, cell + 1 - 2 * core)

    load = pltpu.make_async_copy(snap_hbm, snap, load_sem)
    load.start()

    barrier = pltpu.get_barrier_semaphore()

    def greet(sem, d, axis):
        target = {
            "x": lambda: device((x + d) % 4, y, z, core),
            "y": lambda: device(x, (y + d) % 8, z, core),
            "z": lambda: device(x, y, (z + d) % 8, core),
        }[axis]()
        pl.semaphore_signal(sem, inc=1, device_id=target, device_id_type=MESH)

    for d in range(1, 4):
        greet(barrier, d, "x")
    for d in range(1, 8):
        greet(barrier, d, "y")
        greet(barrier, d, "z")
    pl.semaphore_signal(barrier, inc=1, device_id=peer, device_id_type=MESH)

    load.wait()
    scale = jnp.sqrt(jnp.full((1, SNAP), density_ref[z], jnp.float32))
    for q in range(4):
        block = snap[pl.ds(q * QUARTER, QUARTER), :].astype(jnp.float32) * scale
        turned[q] = block.astype(jnp.bfloat16).T
    own[ylo] = turned[ylo]
    pl.semaphore_wait(barrier, 18)

    def y_copy(q):
        return copy_to(
            turned.at[q], own.at[ylo], y_send.at[q], y_recv.at[ylo], device(x, y_base + q, z, core)
        )

    def y_arrival(q):
        return copy_to(turned.at[q], own.at[q], y_send.at[q], y_recv.at[q], device(x, y_base + q, z, core))

    def other_y(d):
        return (ylo + d) % 4

    for d in (1, 2, 3):
        y_copy(other_y(d)).start()

    half = x // 2
    half_next2 = ((x + 2) % 4) // 2

    def x1_copy(q):
        return copy_to(
            own.at[q], next1.at[q], x1_send.at[q], x1_recv.at[q], device((x + 3) % 4, y, z, core)
        )

    def x2_copy(q):
        lanes = pl.ds(pl.multiple_of(half_next2 * HALF, HALF), HALF)
        return copy_to(
            own.at[q, :, lanes], next2.at[q], x2_send.at[q], x2_recv.at[q], device((x + 2) % 4, y, z, core)
        )

    x1_copy(ylo).start()
    x2_copy(ylo).start()

    for d in range(1, 8):
        greet(plane_sem, d, "y")

    for d in (1, 2, 3):
        q = other_y(d)
        y_arrival(q).wait_recv()
        x1_copy(q).start()
        x2_copy(q).start()

    pl.semaphore_wait(plane_sem, 7)
    for d in range(1, 4):
        greet(all_sem, d, "x")

    def multiply(g, left, right):
        product = lax.dot_general(
            left, right, (((1,), (1,)), ((), ())), preferred_element_type=jnp.float32
        )
        for n in range(8):
            for h in range(2):
                for t in range(4):
                    part[g, h, t // 2, n, t % 2] = product[
                        n * 64 + h * 32 : n * 64 + h * 32 + 32, t * 128 : t * 128 + 128
                    ]

    def core_copy(g):
        return copy_to(part.at[g, 1 - core], peer_part.at[g], core_send.at[g], core_recv.at[g], peer)

    def ring_copy(g, colour, d):
        if colour == 0:
            here, there = z, (z + d) % 8
            target = device(x, y, there, core)
        else:
            here, there = y, (y + d) % 8
            target = device(x, there, z, core)
        return copy_to(
            part.at[g, core, colour, there],
            arrived.at[g, colour, here],
            ring_send.at[g, colour],
            ring_recv.at[g, colour],
            target,
        )

    def spread(g):
        core_copy(g).wait_recv()
        part[g, core] = part[g, core] + peer_part[g]

        @pl.loop(1, 8)
        def _(d):
            ring_copy(g, 0, d).start()
            ring_copy(g, 1, d).start()

    left = own[...].reshape(512, QUARTER)
    multiply(0, left, left)
    core_copy(0).start()

    for q in range(4):
        x1_copy(q).wait_recv()
    multiply(1, own[...].reshape(512, QUARTER), next1[...].reshape(512, QUARTER))
    core_copy(1).start()
    spread(0)

    for q in range(4):
        x2_copy(q).wait_recv()
    lanes = pl.ds(pl.multiple_of(half * HALF, HALF), HALF)
    multiply(2, own[:, :, lanes].reshape(512, HALF), next2[...].reshape(512, HALF))
    core_copy(2).start()
    spread(1)
    spread(2)
    pl.semaphore_wait(all_sem, 3)

    def cross_copy(colour, d):
        if colour == 0:
            here, there = y, (y + d) % 8
            target = device(x, there, z, core)
        else:
            here, there = z, (z + d) % 8
            target = device(x, y, there, core)
        return copy_to(
            total.at[colour, there], crossed.at[colour, here], cross_send.at[colour], cross_recv.at[colour], target
        )

    for colour in range(2):
        here = z if colour == 0 else y
        for g in range(3):
            seven = arrived.at[g, colour, pl.ds(0, 7)]
            copy_to(seven, seven, ring_send.at[g, colour], ring_recv.at[g, colour], peer).wait_recv()
            acc = part[g, core, colour, here]
            for d in range(1, 8):
                acc = acc + arrived[g, colour, (here + d) % 8]
            total[colour, :, g] = acc.reshape(8, 8, 128)

        @pl.loop(1, 8)
        def _(d):
            cross_copy(colour, d).start()

    def tile_copies(colour, g, act):
        where, index = (z, y) if colour == 0 else (y, z)
        row = x * 4 + where // 2
        column = ((x + g) % 4) * 4 + 2 * colour + index // 4
        targets = [(0, row, 2 * column + core)]
        if g > 0:
            targets.append((1, column, 2 * row + core))
        for kind, to_grp, to_cell in targets:
            here = jnp.logical_and(to_grp == grp, to_cell == cell)
            src = piece.at[colour, g]
            dst = mine.at[kind, where % 2, index % 4]
            act(src, dst, kind, here, (to_grp, to_cell))

    def start_tile(src, dst, kind, here, target):
        @pl.when(here)
        def _():
            pltpu.make_async_copy(src, dst, tile_recv.at[kind]).start()

        @pl.when(jnp.logical_not(here))
        def _():
            copy_to(src, dst, tile_send, tile_recv.at[kind], target).start()

    def finish_tile(src, dst, kind, here, target):
        @pl.when(jnp.logical_not(here))
        def _():
            copy_to(src, dst, tile_send, tile_recv.at[kind], target).wait_send()

    for colour in range(2):
        here = y if colour == 0 else z
        seven = crossed.at[colour, pl.ds(0, 7)]
        copy_to(seven, seven, cross_send.at[colour], cross_recv.at[colour], peer).wait_recv()
        acc = total[colour, here]
        for d in range(1, 8):
            acc = acc + crossed[colour, (here + d) % 8]
        piece[colour] = acc
        for g in range(3):
            tile_copies(colour, g, start_tile)

    apart = (cell // 8 - x) % 4
    for kind in range(2):
        used = apart != 3 if kind == 0 else apart >= 2

        @pl.when(used)
        def _(kind=kind):
            whole = mine.at[kind]
            copy_to(whole, whole, tile_send, tile_recv.at[kind], peer).wait_recv()

        @pl.when(jnp.logical_not(used))
        def _(kind=kind):
            mine[kind] = jnp.zeros_like(mine[kind])

    last = copy_to(mine, other, last_send, last_recv, peer)
    last.start()

    for q in (1, 2, 3):
        y_copy(other_y(q)).wait_send()
    for q in range(4):
        x1_copy(q).wait_send()
        x2_copy(q).wait_send()
    for g in range(3):
        core_copy(g).wait_send()
        for colour in range(2):
            seven = arrived.at[g, colour, pl.ds(0, 7)]
            copy_to(seven, seven, ring_send.at[g, colour], ring_recv.at[g, colour], peer).wait_send()
            tile_copies(colour, g, finish_tile)
    for colour in range(2):
        seven = crossed.at[colour, pl.ds(0, 7)]
        copy_to(seven, seven, cross_send.at[colour], cross_recv.at[colour], peer).wait_send()

    last.wait()
    first = core == 0
    low = jnp.where(first, mine[...], other[...]).reshape(2, 2, 32, 128)
    high = jnp.where(first, other[...], mine[...]).reshape(2, 2, 32, 128)

    def whole_tile(kind):
        return jnp.concatenate([low[kind, 0], high[kind, 0], low[kind, 1], high[kind, 1]], axis=0)

    full = (whole_tile(0) + whole_tile(1).T) * (1.0 / CELLS)
    out_ref[...] = jnp.where(first, full[:, :64], full[:, 64:])


def body(snapshots, density):
    f32, bf16, dma = jnp.float32, jnp.bfloat16, pltpu.SemaphoreType.DMA
    return pl.pallas_call(
        kernel,
        out_shape=jax.ShapeDtypeStruct((128, 64), f32),
        in_specs=[pl.BlockSpec(memory_space=pl.ANY), pl.BlockSpec(memory_space=pltpu.SMEM)],
        out_specs=pl.BlockSpec(memory_space=pltpu.VMEM),
        scratch_shapes=[
            pltpu.VMEM((SLAB, SNAP), bf16),
            pltpu.VMEM((4, SNAP, QUARTER), bf16),
            pltpu.VMEM((4, SNAP, QUARTER), bf16),
            pltpu.VMEM((4, SNAP, QUARTER), bf16),
            pltpu.VMEM((4, SNAP, HALF), bf16),
            pltpu.VMEM((3, 2, 2, 8, 2, 32, 128), f32),
            pltpu.VMEM((3, 2, 8, 2, 32, 128), f32),
            pltpu.VMEM((3, 2, 8, 2, 32, 128), f32),
            pltpu.VMEM((2, 8, 3, 8, 128), f32),
            pltpu.VMEM((2, 8, 3, 8, 128), f32),
            pltpu.VMEM((2, 3, 8, 128), f32),
            pltpu.VMEM((2, 2, 4, 8, 128), f32),
            pltpu.VMEM((2, 2, 4, 8, 128), f32),
            dma, dma((4,)), dma((4,)), dma((4,)), dma((4,)), dma((4,)), dma((4,)), dma((3,)), dma((3,)),
            dma((3, 2)), dma((3, 2)), dma((2,)), dma((2,)), dma, dma((2,)), dma, dma,
            pltpu.SemaphoreType.REGULAR, pltpu.SemaphoreType.REGULAR,
        ],
        compiler_params=pltpu.CompilerParams(
            collective_id=0, has_side_effects=True, vmem_limit_bytes=40 * 2**20
        ),
        cost_estimate=pl.CostEstimate(flops=10**9, bytes_accessed=10**6, transcendentals=0),
    )(snapshots, density)


def solution(mesh):
    in_specs = (P("cell", "grp"), P())
    return jax.shard_map(body, mesh=mesh, in_specs=in_specs, out_specs=P("grp", "cell"), check_vma=False)
```

```python
import jax
import jax.numpy as jnp
from jax import lax
from jax.experimental import pallas as pl
from jax.experimental.pallas import tpu as pltpu
from jax.sharding import PartitionSpec as P

MESH = pl.DeviceIdType.MESH
CELLS = 98304
SLAB = 3072
QUARTER = SLAB // 4
CHUNKS = 3
AHEAD = 1
WIDE = QUARTER // CHUNKS
NARROW = WIDE // 2
SNAP = 128


def device(x, y, z, core):
    return x * 4 + y % 4, (z * 2 + y // 4) * 2 + core


def copy_to(src, dst, send, recv, target):
    return pltpu.make_async_remote_copy(
        src_ref=src, dst_ref=dst, send_sem=send, recv_sem=recv, device_id=target, device_id_type=MESH
    )


def kernel(
    snap_hbm, density_ref, out_ref,
    snap, turned, own, next1, passing, next2, part, peer_part, arrived, total, crossed, piece, mine, other,
    load_sem, y_send, y_recv, x1_send, x1_recv, pass_send, pass_recv, x2_send, x2_recv, core_send, core_recv,
    ring_send, ring_recv, cross_send, cross_recv, tile_send, tile_recv, last_send, last_recv, plane_sem, all_sem,
):
    grp, cell = lax.axis_index("grp"), lax.axis_index("cell")
    x, ylo, z, core = grp // 4, grp % 4, cell // 4, cell % 2
    y = (cell // 2) % 2 * 4 + ylo
    y_base = y - ylo
    peer = (grp, cell + 1 - 2 * core)

    load = pltpu.make_async_copy(snap_hbm, snap, load_sem)
    load.start()

    barrier = pltpu.get_barrier_semaphore()

    def greet(sem, d, axis):
        target = {
            "x": lambda: device((x + d) % 4, y, z, core),
            "y": lambda: device(x, (y + d) % 8, z, core),
            "z": lambda: device(x, y, (z + d) % 8, core),
        }[axis]()
        pl.semaphore_signal(sem, inc=1, device_id=target, device_id_type=MESH)

    for d in range(1, 4):
        greet(barrier, d, "x")
    for d in range(1, 8):
        greet(barrier, d, "y")
        greet(barrier, d, "z")
    pl.semaphore_signal(barrier, inc=1, device_id=peer, device_id_type=MESH)

    load.wait()
    scale = jnp.sqrt(jnp.full((1, SNAP), density_ref[z], jnp.float32))
    for q in range(4):
        for c in range(CHUNKS):
            block = snap[pl.ds(q * QUARTER + c * WIDE, WIDE), :].astype(jnp.float32) * scale
            turned[q, c] = block.astype(jnp.bfloat16).T
    for c in range(CHUNKS):
        own[c, ylo] = turned[ylo, c]
    pl.semaphore_wait(barrier, 18)

    def other_y(d):
        return (ylo + d) % 4

    def y_copy(c, q):
        return copy_to(
            turned.at[q, c], own.at[c, ylo], y_send.at[c, q], y_recv.at[c, ylo], device(x, y_base + q, z, core)
        )

    def y_arrival(c, q):
        return copy_to(
            turned.at[q, c], own.at[c, q], y_send.at[c, q], y_recv.at[c, q], device(x, y_base + q, z, core)
        )

    half = x // 2
    half_next2 = ((x + 2) % 4) // 2

    def x1_copy(c):
        return copy_to(own.at[c], next1.at[c], x1_send.at[c], x1_recv.at[c], device((x + 3) % 4, y, z, core))

    def pass_copy(c):
        lanes = pl.ds(pl.multiple_of(half_next2 * NARROW, NARROW), NARROW)
        return copy_to(
            own.at[c, :, :, lanes], passing.at[c], pass_send.at[c], pass_recv.at[c], device((x + 1) % 4, y, z, core)
        )

    def x2_copy(c):
        return copy_to(
            passing.at[c], next2.at[c], x2_send.at[c], x2_recv.at[c], device((x + 1) % 4, y, z, core)
        )

    for c in range(AHEAD):
        for d in (1, 2, 3):
            y_copy(c, other_y(d)).start()

    for d in range(1, 8):
        greet(plane_sem, d, "y")

    for c in range(CHUNKS):
        for d in (1, 2, 3):
            y_arrival(c, other_y(d)).wait_recv()
        if c + AHEAD < CHUNKS:
            for d in (1, 2, 3):
                y_copy(c, other_y(d)).wait_send()
            for d in (1, 2, 3):
                y_copy(c + AHEAD, other_y(d)).start()
        x1_copy(c).start()
        pass_copy(c).start()
        if c > 0:
            pass_copy(c - 1).wait_recv()
            x2_copy(c - 1).start()

    pl.semaphore_wait(plane_sem, 7)
    for d in range(1, 4):
        greet(all_sem, d, "x")

    def multiply(g, left, right):
        product = None
        for c in range(CHUNKS):
            term = lax.dot_general(
                left(c), right(c), (((1,), (1,)), ((), ())), preferred_element_type=jnp.float32
            )
            product = term if product is None else product + term
        for n in range(8):
            for h in range(2):
                for t in range(4):
                    part[g, h, t // 2, n, t % 2] = product[
                        n * 64 + h * 32 : n * 64 + h * 32 + 32, t * 128 : t * 128 + 128
                    ]

    def core_copy(g):
        return copy_to(part.at[g, 1 - core], peer_part.at[g], core_send.at[g], core_recv.at[g], peer)

    def ring_copy(g, colour, d):
        if colour == 0:
            here, there = z, (z + d) % 8
            target = device(x, y, there, core)
        else:
            here, there = y, (y + d) % 8
            target = device(x, there, z, core)
        return copy_to(
            part.at[g, core, colour, there],
            arrived.at[g, colour, here],
            ring_send.at[g, colour],
            ring_recv.at[g, colour],
            target,
        )

    def spread(g):
        core_copy(g).wait_recv()
        part[g, core] = part[g, core] + peer_part[g]

        @pl.loop(1, 8)
        def _(d):
            ring_copy(g, 0, d).start()
            ring_copy(g, 1, d).start()

    def mine_at(c):
        return own[c].reshape(512, WIDE)

    multiply(0, mine_at, mine_at)
    core_copy(0).start()

    pass_copy(CHUNKS - 1).wait_recv()
    x2_copy(CHUNKS - 1).start()
    spread(0)

    for c in range(CHUNKS):
        x1_copy(c).wait_recv()
    multiply(1, mine_at, lambda c: next1[c].reshape(512, WIDE))
    core_copy(1).start()

    for c in range(CHUNKS):
        x2_copy(c).wait_recv()
    lanes = pl.ds(pl.multiple_of(half * NARROW, NARROW), NARROW)
    multiply(2, lambda c: own[c, :, :, lanes].reshape(512, NARROW), lambda c: next2[c].reshape(512, NARROW))
    core_copy(2).start()
    spread(1)
    spread(2)
    pl.semaphore_wait(all_sem, 3)

    def cross_copy(colour, d):
        if colour == 0:
            here, there = y, (y + d) % 8
            target = device(x, there, z, core)
        else:
            here, there = z, (z + d) % 8
            target = device(x, y, there, core)
        return copy_to(
            total.at[colour, there], crossed.at[colour, here], cross_send.at[colour], cross_recv.at[colour], target
        )

    for colour in range(2):
        here = z if colour == 0 else y
        for g in range(3):
            seven = arrived.at[g, colour, pl.ds(0, 7)]
            copy_to(seven, seven, ring_send.at[g, colour], ring_recv.at[g, colour], peer).wait_recv()
            acc = part[g, core, colour, here]
            for d in range(1, 8):
                acc = acc + arrived[g, colour, (here + d) % 8]
            total[colour, :, g] = acc.reshape(8, 8, 128)

        @pl.loop(1, 8)
        def _(d):
            cross_copy(colour, d).start()

    def tile_copies(colour, g, act):
        where, index = (z, y) if colour == 0 else (y, z)
        row = x * 4 + where // 2
        column = ((x + g) % 4) * 4 + 2 * colour + index // 4
        targets = [(0, row, 2 * column + core)]
        if g > 0:
            targets.append((1, column, 2 * row + core))
        for kind, to_grp, to_cell in targets:
            here = jnp.logical_and(to_grp == grp, to_cell == cell)
            src = piece.at[colour, g]
            dst = mine.at[kind, where % 2, index % 4]
            act(src, dst, kind, here, (to_grp, to_cell))

    def start_tile(src, dst, kind, here, target):
        @pl.when(here)
        def _():
            pltpu.make_async_copy(src, dst, tile_recv.at[kind]).start()

        @pl.when(jnp.logical_not(here))
        def _():
            copy_to(src, dst, tile_send, tile_recv.at[kind], target).start()

    def finish_tile(src, dst, kind, here, target):
        @pl.when(jnp.logical_not(here))
        def _():
            copy_to(src, dst, tile_send, tile_recv.at[kind], target).wait_send()

    for colour in range(2):
        here = y if colour == 0 else z
        seven = crossed.at[colour, pl.ds(0, 7)]
        copy_to(seven, seven, cross_send.at[colour], cross_recv.at[colour], peer).wait_recv()
        acc = total[colour, here]
        for d in range(1, 8):
            acc = acc + crossed[colour, (here + d) % 8]
        piece[colour] = acc
        for g in range(3):
            tile_copies(colour, g, start_tile)

    apart = (cell // 8 - x) % 4
    for kind in range(2):
        used = apart != 3 if kind == 0 else apart >= 2

        @pl.when(used)
        def _(kind=kind):
            whole = mine.at[kind]
            copy_to(whole, whole, tile_send, tile_recv.at[kind], peer).wait_recv()

        @pl.when(jnp.logical_not(used))
        def _(kind=kind):
            mine[kind] = jnp.zeros_like(mine[kind])

    last = copy_to(mine, other, last_send, last_recv, peer)
    last.start()

    for c in range(CHUNKS):
        if c + AHEAD >= CHUNKS:
            for d in (1, 2, 3):
                y_copy(c, other_y(d)).wait_send()
        x1_copy(c).wait_send()
        pass_copy(c).wait_send()
        x2_copy(c).wait_send()
    for g in range(3):
        core_copy(g).wait_send()
        for colour in range(2):
            seven = arrived.at[g, colour, pl.ds(0, 7)]
            copy_to(seven, seven, ring_send.at[g, colour], ring_recv.at[g, colour], peer).wait_send()
            tile_copies(colour, g, finish_tile)
    for colour in range(2):
        seven = crossed.at[colour, pl.ds(0, 7)]
        copy_to(seven, seven, cross_send.at[colour], cross_recv.at[colour], peer).wait_send()

    last.wait()
    first = core == 0
    low = jnp.where(first, mine[...], other[...]).reshape(2, 2, 32, 128)
    high = jnp.where(first, other[...], mine[...]).reshape(2, 2, 32, 128)

    def whole_tile(kind):
        return jnp.concatenate([low[kind, 0], high[kind, 0], low[kind, 1], high[kind, 1]], axis=0)

    full = (whole_tile(0) + whole_tile(1).T) * (1.0 / CELLS)
    out_ref[...] = jnp.where(first, full[:, :64], full[:, 64:])


def body(snapshots, density):
    f32, bf16, dma = jnp.float32, jnp.bfloat16, pltpu.SemaphoreType.DMA
    return pl.pallas_call(
        kernel,
        out_shape=jax.ShapeDtypeStruct((128, 64), f32),
        in_specs=[pl.BlockSpec(memory_space=pl.ANY), pl.BlockSpec(memory_space=pltpu.SMEM)],
        out_specs=pl.BlockSpec(memory_space=pltpu.VMEM),
        scratch_shapes=[
            pltpu.VMEM((SLAB, SNAP), bf16),
            pltpu.VMEM((4, CHUNKS, SNAP, WIDE), bf16),
            pltpu.VMEM((CHUNKS, 4, SNAP, WIDE), bf16),
            pltpu.VMEM((CHUNKS, 4, SNAP, WIDE), bf16),
            pltpu.VMEM((CHUNKS, 4, SNAP, NARROW), bf16),
            pltpu.VMEM((CHUNKS, 4, SNAP, NARROW), bf16),
            pltpu.VMEM((3, 2, 2, 8, 2, 32, 128), f32),
            pltpu.VMEM((3, 2, 8, 2, 32, 128), f32),
            pltpu.VMEM((3, 2, 8, 2, 32, 128), f32),
            pltpu.VMEM((2, 8, 3, 8, 128), f32),
            pltpu.VMEM((2, 8, 3, 8, 128), f32),
            pltpu.VMEM((2, 3, 8, 128), f32),
            pltpu.VMEM((2, 2, 4, 8, 128), f32),
            pltpu.VMEM((2, 2, 4, 8, 128), f32),
            dma, dma((CHUNKS, 4)), dma((CHUNKS, 4)), *[dma((CHUNKS,))] * 6, dma((3,)), dma((3,)),
            dma((3, 2)), dma((3, 2)), dma((2,)), dma((2,)), dma, dma((2,)), dma, dma,
            pltpu.SemaphoreType.REGULAR, pltpu.SemaphoreType.REGULAR,
        ],
        compiler_params=pltpu.CompilerParams(
            collective_id=0, has_side_effects=True, vmem_limit_bytes=60 * 2**20
        ),
        cost_estimate=pl.CostEstimate(flops=10**9, bytes_accessed=10**6, transcendentals=0),
    )(snapshots, density)


def solution(mesh):
    in_specs = (P("cell", "grp"), P())
    return jax.shard_map(body, mesh=mesh, in_specs=in_specs, out_specs=P("grp", "cell"), check_vma=False)
```

```python
import jax
import jax.numpy as jnp
from jax import lax
from jax.experimental import pallas as pl
from jax.experimental.pallas import tpu as pltpu
from jax.sharding import PartitionSpec as P

MESH = pl.DeviceIdType.MESH
CELLS = 98304
SLAB = 3072
QUARTER = SLAB // 4
CHUNKS = 6
HALF = CHUNKS // 2
AHEAD = 2
WIDE = QUARTER // CHUNKS
SNAP = 128


def device(x, y, z, core):
    return x * 4 + y % 4, (z * 2 + y // 4) * 2 + core


def copy_to(src, dst, send, recv, target):
    return pltpu.make_async_remote_copy(
        src_ref=src, dst_ref=dst, send_sem=send, recv_sem=recv, device_id=target, device_id_type=MESH
    )


def kernel(
    snap_hbm, density_ref, out_ref,
    snap, turned, own, next1, passing, next2, part, peer_part, between, arrived, total, crossed, piece, mine, other,
    load_sem, y_send, y_recv, x1_send, x1_recv, pass_send, pass_recv, x2_send, x2_recv, core_send, core_recv,
    line_send, between_recv, arrived_recv, cross_send, cross_recv, tile_send, tile_recv, last_send, last_recv, plane_sem, all_sem,
):
    grp, cell = lax.axis_index("grp"), lax.axis_index("cell")
    x, ylo, z, core = grp // 4, grp % 4, cell // 4, cell % 2
    y = (cell // 2) % 2 * 4 + ylo
    y_base = y - ylo
    peer = (grp, cell + 1 - 2 * core)

    load = pltpu.make_async_copy(snap_hbm, snap, load_sem)
    load.start()

    barrier = pltpu.get_barrier_semaphore()

    def greet(sem, d, axis):
        target = {
            "x": lambda: device((x + d) % 4, y, z, core),
            "y": lambda: device(x, (y + d) % 8, z, core),
            "z": lambda: device(x, y, (z + d) % 8, core),
        }[axis]()
        pl.semaphore_signal(sem, inc=1, device_id=target, device_id_type=MESH)

    for d in range(1, 4):
        greet(barrier, d, "x")
    for d in range(1, 8):
        greet(barrier, d, "y")
        greet(barrier, d, "z")
    pl.semaphore_signal(barrier, inc=1, device_id=peer, device_id_type=MESH)

    half = x // 2
    first_chunk = (1 - half) * HALF

    def chunk(n):
        return (n + first_chunk) % CHUNKS

    load.wait()
    scale = jnp.sqrt(jnp.full((1, SNAP), density_ref[z], jnp.float32))

    def weigh(c):
        for q in range(4):
            rows = pl.ds(pl.multiple_of(q * QUARTER + c * WIDE, WIDE), WIDE)
            turned[q, c] = (snap[rows, :].astype(jnp.float32) * scale).astype(jnp.bfloat16).T
        own[c, ylo] = turned[ylo, c]

    def other_y(d):
        return (ylo + d) % 4

    def y_copy(c, q):
        return copy_to(
            turned.at[q, c], own.at[c, ylo], y_send.at[c, q], y_recv.at[c, ylo], device(x, y_base + q, z, core)
        )

    def y_arrival(c, q):
        return copy_to(
            turned.at[q, c], own.at[c, q], y_send.at[c, q], y_recv.at[c, q], device(x, y_base + q, z, core)
        )

    def x1_copy(c):
        return copy_to(own.at[c], next1.at[c], x1_send.at[c], x1_recv.at[c], device((x + 3) % 4, y, z, core))

    def pass_copy(n):
        return copy_to(
            own.at[chunk(n)], passing.at[n], pass_send.at[n], pass_recv.at[n], device((x + 1) % 4, y, z, core)
        )

    def x2_copy(n):
        return copy_to(
            passing.at[n], next2.at[n], x2_send.at[n], x2_recv.at[n], device((x + 1) % 4, y, z, core)
        )

    def start_y(n):
        for d in (1, 2, 3):
            y_copy(chunk(n), other_y(d)).start()

    for n in range(AHEAD):
        weigh(chunk(n))
    pl.semaphore_wait(barrier, 18)
    for n in range(AHEAD):
        start_y(n)
    for n in range(AHEAD, CHUNKS):
        weigh(chunk(n))

    for d in range(1, 8):
        greet(plane_sem, d, "y")

    for n in range(CHUNKS):
        for d in (1, 2, 3):
            y_arrival(chunk(n), other_y(d)).wait_recv()
        if n + AHEAD < CHUNKS:
            for d in (1, 2, 3):
                y_copy(chunk(n), other_y(d)).wait_send()
            start_y(n + AHEAD)
        x1_copy(chunk(n)).start()
        if n < HALF:
            pass_copy(n).start()
        if 2 <= n < HALF + 2:
            pass_copy(n - 2).wait_recv()
            x2_copy(n - 2).start()

    pl.semaphore_wait(plane_sem, 7)
    for d in range(1, 4):
        greet(all_sem, d, "x")

    def multiply(g, chunks, left, right):
        product = None
        for c in range(chunks):
            term = lax.dot_general(
                left(c).reshape(512, WIDE), right(c).reshape(512, WIDE), (((1,), (1,)), ((), ())),
                preferred_element_type=jnp.float32,
            )
            product = term if product is None else product + term
        for n in range(8):
            for h in range(2):
                for t in range(4):
                    part[g, h, t // 2, n, t % 2] = product[
                        n * 64 + h * 32 : n * 64 + h * 32 + 32, t * 128 : t * 128 + 128
                    ]

    def core_copy(g):
        return copy_to(part.at[g, 1 - core], peer_part.at[g], core_send.at[g], core_recv.at[g], peer)

    def place(colour):
        return z if colour == 0 else y

    def at_line(colour, d):
        there = (place(colour) + d + 8) % 8
        return there, device(x, y, there, core) if colour == 0 else device(x, there, z, core)

    def line_copy(g, colour, src, dst, recv, target):
        return copy_to(src, dst, line_send.at[g, colour], recv.at[g, colour], target)

    def spread(g):
        core_copy(g).wait_recv()
        part[g, core] = part[g, core] + peer_part[g]
        for colour in range(2):
            terms = part.at[g, core, colour]
            for s, way in ((0, 1), (1, -1)):
                beside, target = at_line(colour, way)
                third, _ = at_line(colour, 3 * way)
                fourth, _ = at_line(colour, 4)
                _, target2 = at_line(colour, 2 * way)
                slot = between.at[g, colour, s]
                line_copy(g, colour, terms.at[third], slot.at[pl.ds(0, 2)], between_recv, target).start()
                line_copy(g, colour, terms.at[fourth, s], slot.at[2], between_recv, target2).start()
        for colour in range(2):
            terms = part.at[g, core, colour]
            for s, way in ((0, 1), (1, -1)):
                beside, target = at_line(colour, way)
                line_copy(g, colour, terms.at[beside], arrived.at[g, colour, s], arrived_recv, target).start()

    def send_on(g):
        for colour in range(2):
            terms = part.at[g, core, colour]
            whole = between.at[g, colour]
            line_copy(g, colour, whole, whole, between_recv, peer).wait_recv()
            for s, way in ((0, 1), (1, -1)):
                there, target = at_line(colour, 2 * way)
                terms[there] = terms[there] + between[g, colour, s, :2]
                terms[there, s] = terms[there, s] + between[g, colour, s, 2]
                line_copy(g, colour, terms.at[there], arrived.at[g, colour, 2 + s], arrived_recv, target).start()

    multiply(0, CHUNKS, lambda c: own[c], lambda c: own[c])
    core_copy(0).start()

    for n in range(HALF):
        x2_copy(n).wait_recv()
    multiply(2, HALF, lambda n: own[half * HALF + n], lambda n: next2[n])
    core_copy(2).start()
    spread(0)
    spread(2)

    for c in range(CHUNKS):
        x1_copy(c).wait_recv()
    multiply(1, CHUNKS, lambda c: own[c], lambda c: next1[c])
    core_copy(1).start()
    spread(1)
    send_on(0)
    send_on(2)
    send_on(1)
    pl.semaphore_wait(all_sem, 3)

    def cross_copy(colour, d):
        if colour == 0:
            here, there = y, (y + d) % 8
            target = device(x, there, z, core)
        else:
            here, there = z, (z + d) % 8
            target = device(x, y, there, core)
        return copy_to(
            total.at[colour, there], crossed.at[colour, here], cross_send.at[colour], cross_recv.at[colour], target
        )

    for n in range(CHUNKS):
        if n + AHEAD >= CHUNKS:
            for d in (1, 2, 3):
                y_copy(chunk(n), other_y(d)).wait_send()
        x1_copy(n).wait_send()
        if n < HALF:
            pass_copy(n).wait_send()
            x2_copy(n).wait_send()
    for g in range(3):
        core_copy(g).wait_send()

    for colour in range(2):
        here = z if colour == 0 else y
        for g in range(3):
            whole = arrived.at[g, colour]
            line_copy(g, colour, whole, whole, arrived_recv, peer).wait_recv()
            acc = part[g, core, colour, here]
            for d in range(4):
                acc = acc + arrived[g, colour, d]
            total[colour, :, g] = acc.reshape(8, 8, 128)

        @pl.loop(1, 8)
        def _(d):
            cross_copy(colour, d).start()

    def tile_copies(colour, g, act):
        where, index = (z, y) if colour == 0 else (y, z)
        row = x * 4 + where // 2
        column = ((x + g) % 4) * 4 + 2 * colour + index // 4
        targets = [(0, row, 2 * column + core)]
        if g > 0:
            targets.append((1, column, 2 * row + core))
        for kind, to_grp, to_cell in targets:
            here = jnp.logical_and(to_grp == grp, to_cell == cell)
            src = piece.at[colour, g]
            dst = mine.at[kind, where % 2, index % 4]
            act(src, dst, kind, here, (to_grp, to_cell))

    def start_tile(src, dst, kind, here, target):
        @pl.when(here)
        def _():
            pltpu.make_async_copy(src, dst, tile_recv.at[kind]).start()

        @pl.when(jnp.logical_not(here))
        def _():
            copy_to(src, dst, tile_send, tile_recv.at[kind], target).start()

    def finish_tile(src, dst, kind, here, target):
        @pl.when(jnp.logical_not(here))
        def _():
            copy_to(src, dst, tile_send, tile_recv.at[kind], target).wait_send()

    for colour in range(2):
        here = y if colour == 0 else z
        seven = crossed.at[colour, pl.ds(0, 7)]
        copy_to(seven, seven, cross_send.at[colour], cross_recv.at[colour], peer).wait_recv()
        acc = total[colour, here]
        for d in range(1, 8):
            acc = acc + crossed[colour, (here + d) % 8]
        piece[colour] = acc
        for g in range(3):
            tile_copies(colour, g, start_tile)

    apart = (cell // 8 - x) % 4
    for kind in range(2):
        used = apart != 3 if kind == 0 else apart >= 2

        @pl.when(used)
        def _(kind=kind):
            whole = mine.at[kind]
            copy_to(whole, whole, tile_send, tile_recv.at[kind], peer).wait_recv()

        @pl.when(jnp.logical_not(used))
        def _(kind=kind):
            mine[kind] = jnp.zeros_like(mine[kind])

    last = copy_to(mine, other, last_send, last_recv, peer)
    last.start()

    for g in range(3):
        for colour in range(2):
            seven = part.at[g, core, colour, pl.ds(0, 7)]
            line_copy(g, colour, seven, seven, arrived_recv, peer).wait_send()
            tile_copies(colour, g, finish_tile)
    for colour in range(2):
        seven = crossed.at[colour, pl.ds(0, 7)]
        copy_to(seven, seven, cross_send.at[colour], cross_recv.at[colour], peer).wait_send()

    last.wait()
    first = core == 0
    low = jnp.where(first, mine[...], other[...]).reshape(2, 2, 32, 128)
    high = jnp.where(first, other[...], mine[...]).reshape(2, 2, 32, 128)

    def whole_tile(kind):
        return jnp.concatenate([low[kind, 0], high[kind, 0], low[kind, 1], high[kind, 1]], axis=0)

    full = (whole_tile(0).T + whole_tile(1)) * (1.0 / CELLS)
    out_ref[...] = jnp.where(first, full[:64], full[64:])


def body(snapshots, density):
    f32, bf16, dma = jnp.float32, jnp.bfloat16, pltpu.SemaphoreType.DMA
    return pl.pallas_call(
        kernel,
        out_shape=jax.ShapeDtypeStruct((64, 128), f32),
        in_specs=[pl.BlockSpec(memory_space=pl.ANY), pl.BlockSpec(memory_space=pltpu.SMEM)],
        out_specs=pl.BlockSpec(memory_space=pltpu.VMEM),
        scratch_shapes=[
            pltpu.VMEM((SLAB, SNAP), bf16),
            pltpu.VMEM((4, CHUNKS, SNAP, WIDE), bf16),
            pltpu.VMEM((CHUNKS, 4, SNAP, WIDE), bf16),
            pltpu.VMEM((CHUNKS, 4, SNAP, WIDE), bf16),
            pltpu.VMEM((HALF, 4, SNAP, WIDE), bf16),
            pltpu.VMEM((HALF, 4, SNAP, WIDE), bf16),
            pltpu.VMEM((3, 2, 2, 8, 2, 32, 128), f32),
            pltpu.VMEM((3, 2, 8, 2, 32, 128), f32),
            pltpu.VMEM((3, 2, 2, 3, 32, 128), f32),
            pltpu.VMEM((3, 2, 4, 2, 32, 128), f32),
            pltpu.VMEM((2, 8, 3, 8, 128), f32),
            pltpu.VMEM((2, 8, 3, 8, 128), f32),
            pltpu.VMEM((2, 3, 8, 128), f32),
            pltpu.VMEM((2, 2, 4, 8, 128), f32),
            pltpu.VMEM((2, 2, 4, 8, 128), f32),
            dma, dma((CHUNKS, 4)), dma((CHUNKS, 4)), *[dma((CHUNKS,))] * 2, *[dma((HALF,))] * 4, dma((3,)), dma((3,)),
            dma((3, 2)), dma((3, 2)), dma((3, 2)), dma((2,)), dma((2,)), dma, dma((2,)), dma, dma,
            pltpu.SemaphoreType.REGULAR, pltpu.SemaphoreType.REGULAR,
        ],
        compiler_params=pltpu.CompilerParams(
            collective_id=0, has_side_effects=True, vmem_limit_bytes=60 * 2**20
        ),
        cost_estimate=pl.CostEstimate(flops=10**9, bytes_accessed=10**6, transcendentals=0),
    )(snapshots, density).T


def solution(mesh):
    in_specs = (P("cell", "grp"), P())
    return jax.shard_map(body, mesh=mesh, in_specs=in_specs, out_specs=P("grp", "cell"), check_vma=False)
```

```python
import jax
import jax.numpy as jnp
from jax import lax
from jax.experimental import pallas as pl
from jax.experimental.pallas import tpu as pltpu
from jax.sharding import PartitionSpec as P

MESH = pl.DeviceIdType.MESH
CELLS = 98304
SLAB = 3072
QUARTER = SLAB // 4
CHUNKS = 6
HALF = CHUNKS // 2
AHEAD = 2
EARLY = 4
BATCHES = ((0, 2), (1,))
WIDE = QUARTER // CHUNKS
SNAP = 128


def device(x, y, z, core):
    return x * 4 + y % 4, (z * 2 + y // 4) * 2 + core


def copy_to(src, dst, send, recv, target):
    return pltpu.make_async_remote_copy(
        src_ref=src, dst_ref=dst, send_sem=send, recv_sem=recv, device_id=target, device_id_type=MESH
    )


def kernel(
    snap_hbm, density_ref, out_ref,
    snap, turned, own, next1, passing, next2, part, peer_part, between, arrived, total, crossed, piece, plain, mirror,
    load_sem, y_send, y_recv, x1_send, x1_recv, pass_send, pass_recv, x2_send, x2_recv, core_send, core_recv,
    line_send, between_recv, arrived_recv, cross_send, cross_recv, tile_send, tile_recv, plane_sem, all_sem,
):
    grp, cell = lax.axis_index("grp"), lax.axis_index("cell")
    x, ylo, z, core = grp // 4, grp % 4, cell // 4, cell % 2
    y = (cell // 2) % 2 * 4 + ylo
    y_base = y - ylo
    peer = (grp, cell + 1 - 2 * core)

    load = pltpu.make_async_copy(snap_hbm, snap, load_sem)
    load.start()

    barrier = pltpu.get_barrier_semaphore()

    def greet(sem, d, axis):
        target = {
            "x": lambda: device((x + d) % 4, y, z, core),
            "y": lambda: device(x, (y + d) % 8, z, core),
            "z": lambda: device(x, y, (z + d) % 8, core),
        }[axis]()
        pl.semaphore_signal(sem, inc=1, device_id=target, device_id_type=MESH)

    for d in range(1, 4):
        greet(barrier, d, "x")
    for d in range(1, 8):
        greet(barrier, d, "y")
        greet(barrier, d, "z")
    pl.semaphore_signal(barrier, inc=1, device_id=peer, device_id_type=MESH)

    half = x // 2
    first_chunk = (1 - half) * HALF

    def chunk(n):
        return (n + first_chunk) % CHUNKS

    load.wait()
    scale = jnp.sqrt(jnp.full((1, SNAP), density_ref[z], jnp.float32))

    def weigh(c):
        for q in range(4):
            rows = pl.ds(pl.multiple_of(q * QUARTER + c * WIDE, WIDE), WIDE)
            turned[q, c] = (snap[rows, :].astype(jnp.float32) * scale).astype(jnp.bfloat16).T
        own[c, ylo] = turned[ylo, c]

    def other_y(d):
        return (ylo + d) % 4

    def y_copy(c, q):
        return copy_to(
            turned.at[q, c], own.at[c, ylo], y_send.at[c, q], y_recv.at[c, ylo], device(x, y_base + q, z, core)
        )

    def y_arrival(c, q):
        return copy_to(
            turned.at[q, c], own.at[c, q], y_send.at[c, q], y_recv.at[c, q], device(x, y_base + q, z, core)
        )

    def x1_copy(c):
        return copy_to(own.at[c], next1.at[c], x1_send.at[c], x1_recv.at[c], device((x + 3) % 4, y, z, core))

    def pass_copy(n):
        return copy_to(
            own.at[chunk(n)], passing.at[n], pass_send.at[n], pass_recv.at[n], device((x + 1) % 4, y, z, core)
        )

    def x2_copy(n):
        return copy_to(
            passing.at[n], next2.at[n], x2_send.at[n], x2_recv.at[n], device((x + 1) % 4, y, z, core)
        )

    def start_y(n):
        for d in (1, 2, 3):
            y_copy(chunk(n), other_y(d)).start()

    weigh(chunk(0))
    pl.semaphore_wait(barrier, 18)
    for n in range(CHUNKS):
        if n > 0:
            weigh(chunk(n))
        if n < AHEAD:
            start_y(n)

    for d in range(1, 8):
        greet(plane_sem, d, "y")

    for n in range(CHUNKS):
        for d in (1, 2, 3):
            y_arrival(chunk(n), other_y(d)).wait_recv()
        if n + AHEAD < CHUNKS:
            for d in (1, 2, 3):
                y_copy(chunk(n), other_y(d)).wait_send()
            start_y(n + AHEAD)
        x1_copy(chunk(n)).start()
        if n < HALF:
            pass_copy(n).start()
        if 2 <= n < HALF + 2:
            pass_copy(n - 2).wait_recv()
            x2_copy(n - 2).start()

    pl.semaphore_wait(plane_sem, 7)
    for d in range(1, 4):
        greet(all_sem, d, "x")

    def multiply(g, pairs, more=False):
        left, right = (
            jnp.concatenate([pair[k] for pair in pairs], axis=-1).reshape(512, len(pairs) * WIDE) for k in (0, 1)
        )
        product = lax.dot_general(left, right, (((1,), (1,)), ((), ())), preferred_element_type=jnp.float32)
        for n in range(8):
            for h in range(2):
                for t in range(4):
                    term = product[n * 64 + h * 32 : n * 64 + h * 32 + 32, t * 128 : t * 128 + 128]
                    if more:
                        term = term + part[g, h, t // 2, n, t % 2]
                    part[g, h, t // 2, n, t % 2] = term

    def core_copy(g):
        return copy_to(part.at[g, 1 - core], peer_part.at[g], core_send.at[g], core_recv.at[g], peer)

    def place(colour):
        return z if colour == 0 else y

    def at_line(colour, d):
        there = (place(colour) + d + 8) % 8
        return there, device(x, y, there, core) if colour == 0 else device(x, there, z, core)

    def line_copy(g, colour, src, dst, recv, target):
        return copy_to(src, dst, line_send.at[g, colour], recv.at[g, colour], target)

    def spread(g):
        core_copy(g).wait_recv()
        part[g, core] = part[g, core] + peer_part[g]
        for colour in range(2):
            terms = part.at[g, core, colour]
            for s, way in ((0, 1), (1, -1)):
                beside, target = at_line(colour, way)
                third, _ = at_line(colour, 3 * way)
                fourth, _ = at_line(colour, 4)
                _, target2 = at_line(colour, 2 * way)
                slot = between.at[g, colour, s]
                line_copy(g, colour, terms.at[third], slot.at[pl.ds(0, 2)], between_recv, target).start()
                line_copy(g, colour, terms.at[fourth, s], slot.at[2], between_recv, target2).start()
        for colour in range(2):
            terms = part.at[g, core, colour]
            for s, way in ((0, 1), (1, -1)):
                beside, target = at_line(colour, way)
                line_copy(g, colour, terms.at[beside], arrived.at[g, colour, s], arrived_recv, target).start()

    def send_on(g):
        for colour in range(2):
            terms = part.at[g, core, colour]
            whole = between.at[g, colour]
            line_copy(g, colour, whole, whole, between_recv, peer).wait_recv()
            for s, way in ((0, 1), (1, -1)):
                there, target = at_line(colour, 2 * way)
                terms[there] = terms[there] + between[g, colour, s, :2]
                terms[there, s] = terms[there, s] + between[g, colour, s, 2]
                line_copy(g, colour, terms.at[there], arrived.at[g, colour, 2 + s], arrived_recv, target).start()

    multiply(0, [(own[c], own[c]) for c in range(CHUNKS)])
    core_copy(0).start()

    for n in range(HALF):
        x2_copy(n).wait_recv()
    multiply(2, [(own[half * HALF + n], next2[n]) for n in range(HALF)])
    core_copy(2).start()
    spread(0)

    for n in range(EARLY):
        x1_copy(chunk(n)).wait_recv()
    multiply(1, [(own[chunk(n)], next1[chunk(n)]) for n in range(EARLY)])
    spread(2)
    for n in range(EARLY, CHUNKS):
        x1_copy(chunk(n)).wait_recv()
    multiply(1, [(own[chunk(n)], next1[chunk(n)]) for n in range(EARLY, CHUNKS)], more=True)
    core_copy(1).start()
    spread(1)
    send_on(0)
    send_on(2)
    send_on(1)
    pl.semaphore_wait(all_sem, 3)

    def cross_copy(b, colour, d):
        if colour == 0:
            here, there = y, (y + d) % 8
            target = device(x, there, z, core)
        else:
            here, there = z, (z + d) % 8
            target = device(x, y, there, core)
        groups = pl.ds(2 * b, len(BATCHES[b]))
        return copy_to(
            total.at[colour, there, groups], crossed.at[colour, here, groups],
            cross_send.at[b, colour], cross_recv.at[b, colour], target,
        )

    for n in range(CHUNKS):
        if n + AHEAD >= CHUNKS:
            for d in (1, 2, 3):
                y_copy(chunk(n), other_y(d)).wait_send()
        x1_copy(n).wait_send()
        if n < HALF:
            pass_copy(n).wait_send()
            x2_copy(n).wait_send()
    for g in range(3):
        core_copy(g).wait_send()

    for b, groups in enumerate(BATCHES):
        for colour in range(2):
            for j, g in enumerate(groups):
                whole = arrived.at[g, colour]
                line_copy(g, colour, whole, whole, arrived_recv, peer).wait_recv()
                acc = part[g, core, colour, place(colour)]
                for d in range(4):
                    acc = acc + arrived[g, colour, d]
                total[colour, :, 2 * b + j] = acc.reshape(8, 8, 128)

            @pl.loop(1, 8)
            def _(d):
                cross_copy(b, colour, d).start()

    def tile_copies(colour, b, j, act):
        g = BATCHES[b][j]
        where, index = (z, y) if colour == 0 else (y, z)
        row = x * 4 + where // 2
        column = ((x + g) % 4) * 4 + 2 * colour + index // 4
        targets = [(1, column, 2 * row + where % 2, mirror.at[core, index % 4])]
        if g > 0:
            for k in range(2):
                targets.append((0, row, 2 * column + k, plain.at[where % 2, core, index % 4]))
        for kind, to_grp, to_cell, dst in targets:
            here = jnp.logical_and(to_grp == grp, to_cell == cell)
            act(piece.at[colour, 2 * b + j], dst, kind, here, (to_grp, to_cell))

    def start_tile(src, dst, kind, here, target):
        @pl.when(here)
        def _():
            pltpu.make_async_copy(src, dst, tile_recv.at[kind]).start()

        @pl.when(jnp.logical_not(here))
        def _():
            copy_to(src, dst, tile_send, tile_recv.at[kind], target).start()

    def finish_tile(src, dst, kind, here, target):
        @pl.when(jnp.logical_not(here))
        def _():
            copy_to(src, dst, tile_send, tile_recv.at[kind], target).wait_send()

    for b, groups in enumerate(BATCHES):
        for colour in range(2):
            here = y if colour == 0 else z
            slots = pl.ds(2 * b, len(groups))
            seven = crossed.at[colour, pl.ds(0, 7), slots]
            copy_to(seven, seven, cross_send.at[b, colour], cross_recv.at[b, colour], peer).wait_recv()
            acc = total[colour, here, slots]
            for d in range(1, 8):
                acc = acc + crossed[colour, (here + d) % 8, slots]
            piece[colour, slots] = acc
            for j in range(len(groups)):
                tile_copies(colour, b, j, start_tile)

    for g in range(3):
        for colour in range(2):
            seven = part.at[g, core, colour, pl.ds(0, 7)]
            line_copy(g, colour, seven, seven, arrived_recv, peer).wait_send()
    for b, groups in enumerate(BATCHES):
        for colour in range(2):
            seven = crossed.at[colour, pl.ds(0, 7), pl.ds(2 * b, len(groups))]
            copy_to(seven, seven, cross_send.at[b, colour], cross_recv.at[b, colour], peer).wait_send()
            for j in range(len(groups)):
                tile_copies(colour, b, j, finish_tile)

    apart = (cell // 8 - x) % 4
    has_plain = jnp.logical_or(apart == 1, apart == 2)

    @pl.when(jnp.logical_not(has_plain))
    def _():
        plain[...] = jnp.zeros_like(plain)

    @pl.when(apart == 1)
    def _():
        mirror[...] = jnp.zeros_like(mirror)

    @pl.when(has_plain)
    def _():
        copy_to(plain, plain, tile_send, tile_recv.at[0], peer).wait_recv()

    @pl.when(apart != 1)
    def _():
        copy_to(mirror, mirror, tile_send, tile_recv.at[1], peer).wait_recv()

    turned_back = plain[...].reshape(128, 128).T
    columns = jnp.where(core == 0, turned_back[:64], turned_back[64:])
    out_ref[...] = (columns + mirror[...].reshape(64, 128)) * (1.0 / CELLS)


def body(snapshots, density):
    f32, bf16, dma = jnp.float32, jnp.bfloat16, pltpu.SemaphoreType.DMA
    return pl.pallas_call(
        kernel,
        out_shape=jax.ShapeDtypeStruct((64, 128), f32),
        in_specs=[pl.BlockSpec(memory_space=pl.ANY), pl.BlockSpec(memory_space=pltpu.SMEM)],
        out_specs=pl.BlockSpec(memory_space=pltpu.VMEM),
        scratch_shapes=[
            pltpu.VMEM((SLAB, SNAP), bf16),
            pltpu.VMEM((4, CHUNKS, SNAP, WIDE), bf16),
            pltpu.VMEM((CHUNKS, 4, SNAP, WIDE), bf16),
            pltpu.VMEM((CHUNKS, 4, SNAP, WIDE), bf16),
            pltpu.VMEM((HALF, 4, SNAP, WIDE), bf16),
            pltpu.VMEM((HALF, 4, SNAP, WIDE), bf16),
            pltpu.VMEM((3, 2, 2, 8, 2, 32, 128), f32),
            pltpu.VMEM((3, 2, 8, 2, 32, 128), f32),
            pltpu.VMEM((3, 2, 2, 3, 32, 128), f32),
            pltpu.VMEM((3, 2, 4, 2, 32, 128), f32),
            pltpu.VMEM((2, 8, 3, 8, 128), f32),
            pltpu.VMEM((2, 8, 3, 8, 128), f32),
            pltpu.VMEM((2, 3, 8, 128), f32),
            pltpu.VMEM((2, 2, 4, 8, 128), f32),
            pltpu.VMEM((2, 4, 8, 128), f32),
            dma, dma((CHUNKS, 4)), dma((CHUNKS, 4)), *[dma((CHUNKS,))] * 2, *[dma((HALF,))] * 4, dma((3,)), dma((3,)),
            dma((3, 2)), dma((3, 2)), dma((3, 2)), dma((2, 2)), dma((2, 2)), dma, dma((2,)),
            pltpu.SemaphoreType.REGULAR, pltpu.SemaphoreType.REGULAR,
        ],
        compiler_params=pltpu.CompilerParams(
            collective_id=0, has_side_effects=True, vmem_limit_bytes=60 * 2**20
        ),
        cost_estimate=pl.CostEstimate(flops=10**9, bytes_accessed=10**6, transcendentals=0),
    )(snapshots, density).T


def solution(mesh):
    in_specs = (P("cell", "grp"), P())
    return jax.shard_map(body, mesh=mesh, in_specs=in_specs, out_specs=P("grp", "cell"), check_vma=False)
```

```python
import jax
import jax.numpy as jnp
from jax import lax
from jax.experimental import pallas as pl
from jax.experimental.pallas import tpu as pltpu
from jax.sharding import PartitionSpec as P

MESH = pl.DeviceIdType.MESH
CELLS = 98304
SLAB = 3072
QUARTER = SLAB // 4
CHUNKS = 6
HALF = CHUNKS // 2
AHEAD = 2
EARLY = 4
PIECED = 4
BATCHES = ((0, 2), (1,))
WIDE = QUARTER // CHUNKS
SNAP = 128


def device(x, y, z, core):
    return x * 4 + y % 4, (z * 2 + y // 4) * 2 + core


def copy_to(src, dst, send, recv, target):
    return pltpu.make_async_remote_copy(
        src_ref=src, dst_ref=dst, send_sem=send, recv_sem=recv, device_id=target, device_id_type=MESH
    )


def kernel(
    snap_hbm, density_ref, out_ref,
    snap, turned, own, next1, passing, next2, part, peer_part, between, arrived, total, crossed, piece, plain, mirror,
    load_sem, y_send, y_recv, x1_send, x1_recv, pass_send, pass_recv, x2_send, x2_recv, core_send, core_recv,
    line_send, between_recv, arrived_recv, cross_send, cross_recv, tile_send, tile_recv, plane_sem, all_sem,
):
    grp, cell = lax.axis_index("grp"), lax.axis_index("cell")
    x, ylo, z, core = grp // 4, grp % 4, cell // 4, cell % 2
    y = (cell // 2) % 2 * 4 + ylo
    y_base = y - ylo
    peer = (grp, cell + 1 - 2 * core)

    load = pltpu.make_async_copy(snap_hbm, snap, load_sem)
    load.start()

    barrier = pltpu.get_barrier_semaphore()

    def greet(sem, d, axis):
        target = {
            "x": lambda: device((x + d) % 4, y, z, core),
            "y": lambda: device(x, (y + d) % 8, z, core),
            "z": lambda: device(x, y, (z + d) % 8, core),
        }[axis]()
        pl.semaphore_signal(sem, inc=1, device_id=target, device_id_type=MESH)

    for d in range(1, 4):
        greet(barrier, d, "x")
    for d in range(1, 8):
        greet(barrier, d, "y")
        greet(barrier, d, "z")
    pl.semaphore_signal(barrier, inc=1, device_id=peer, device_id_type=MESH)

    half = x // 2
    first_chunk = (1 - half) * HALF

    def chunk(n):
        return (n + first_chunk) % CHUNKS

    load.wait()
    scale = jnp.sqrt(jnp.full((1, SNAP), density_ref[z], jnp.float32))

    def weigh(c):
        for q in range(4):
            rows = pl.ds(pl.multiple_of(q * QUARTER + c * WIDE, WIDE), WIDE)
            turned[q, c] = (snap[rows, :].astype(jnp.float32) * scale).astype(jnp.bfloat16).T
        own[c, ylo] = turned[ylo, c]

    def other_y(d):
        return (ylo + d) % 4

    def y_copy(c, q):
        return copy_to(
            turned.at[q, c], own.at[c, ylo], y_send.at[c, q], y_recv.at[c, ylo], device(x, y_base + q, z, core)
        )

    def y_arrival(c, q):
        return copy_to(
            turned.at[q, c], own.at[c, q], y_send.at[c, q], y_recv.at[c, q], device(x, y_base + q, z, core)
        )

    def x1_copy(c):
        return copy_to(own.at[c], next1.at[c], x1_send.at[c], x1_recv.at[c], device((x + 3) % 4, y, z, core))

    def x1_piece(c, q):
        return copy_to(
            own.at[c, q], next1.at[c, q], x1_send.at[c], x1_recv.at[c], device((x + 3) % 4, y, z, core)
        )

    def pass_copy(n):
        return copy_to(
            own.at[chunk(n)], passing.at[n], pass_send.at[n], pass_recv.at[n], device((x + 1) % 4, y, z, core)
        )

    def x2_copy(n):
        return copy_to(
            passing.at[n], next2.at[n], x2_send.at[n], x2_recv.at[n], device((x + 1) % 4, y, z, core)
        )

    def start_y(n):
        for d in (1, 2, 3):
            y_copy(chunk(n), other_y(d)).start()

    weigh(chunk(0))
    pl.semaphore_wait(barrier, 18)
    for n in range(CHUNKS):
        if n > 0:
            weigh(chunk(n))
        if n < AHEAD:
            start_y(n)
        if n >= PIECED:
            x1_piece(chunk(n), ylo).start()

    for d in range(1, 8):
        greet(plane_sem, d, "y")

    def multiply(g, colour, pairs, more=False):
        left = jnp.concatenate([pair[0] for pair in pairs], axis=-1).reshape(512, len(pairs) * WIDE)
        right = jnp.concatenate([pair[1] for pair in pairs], axis=-1).reshape(256, len(pairs) * WIDE)
        product = lax.dot_general(left, right, (((1,), (1,)), ((), ())), preferred_element_type=jnp.float32)
        for n in range(8):
            for h in range(2):
                for t in range(2):
                    term = product[n * 64 + h * 32 : n * 64 + h * 32 + 32, t * 128 : t * 128 + 128]
                    if more:
                        term = term + part[g, h, colour, n, t]
                    part[g, h, colour, n, t] = term

    def core_copy(g, colour):
        return copy_to(
            part.at[g, 1 - core, colour], peer_part.at[g, colour],
            core_send.at[g, colour], core_recv.at[g, colour], peer,
        )

    def columns_of(colour):
        return slice(2 * colour, 2 * colour + 2)

    def multiply0(first, last, more):
        for colour in range(2):
            multiply(
                0, colour, [(own[chunk(n)], own[chunk(n), columns_of(colour)]) for n in range(first, last)], more
            )
            if more:
                core_copy(0, colour).start()

    def multiply1(first, last, more):
        for colour in range(2):
            multiply(
                1, colour, [(own[chunk(n)], next1[chunk(n), columns_of(colour)]) for n in range(first, last)], more
            )
            if more:
                core_copy(1, colour).start()

    def multiply2():
        for colour in range(2):
            multiply(2, colour, [(own[half * HALF + n], next2[n, columns_of(colour)]) for n in range(HALF)])
            core_copy(2, colour).start()

    for n in range(CHUNKS):
        for d in (1, 2, 3):
            y_arrival(chunk(n), other_y(d)).wait_recv()
            if n >= PIECED:
                x1_piece(chunk(n), other_y(d)).start()
        if n + AHEAD < CHUNKS:
            for d in (1, 2, 3):
                y_copy(chunk(n), other_y(d)).wait_send()
            start_y(n + AHEAD)
        if n < PIECED:
            x1_copy(chunk(n)).start()
        if n < HALF:
            pass_copy(n).start()
        if 2 <= n < HALF + 2:
            pass_copy(n - 2).wait_recv()
            x2_copy(n - 2).start()
        if n == EARLY:
            multiply0(0, EARLY, False)

    pl.semaphore_wait(plane_sem, 7)
    for d in range(1, 4):
        greet(all_sem, d, "x")

    def place(colour):
        return z if colour == 0 else y

    def at_line(colour, d):
        there = (place(colour) + d + 8) % 8
        return there, device(x, y, there, core) if colour == 0 else device(x, there, z, core)

    def line_copy(g, colour, src, dst, recv, target):
        return copy_to(src, dst, line_send.at[g, colour], recv.at[g, colour], target)

    def spread(g):
        for colour in range(2):
            core_copy(g, colour).wait_recv()
            part[g, core, colour] = part[g, core, colour] + peer_part[g, colour]
            terms = part.at[g, core, colour]
            for s, way in ((0, 1), (1, -1)):
                third, _ = at_line(colour, 3 * way)
                fourth, _ = at_line(colour, 4)
                _, target = at_line(colour, way)
                _, target2 = at_line(colour, 2 * way)
                slot = between.at[g, colour, s]
                line_copy(g, colour, terms.at[third], slot.at[pl.ds(0, 2)], between_recv, target).start()
                line_copy(g, colour, terms.at[fourth, s], slot.at[2], between_recv, target2).start()
        for colour in range(2):
            terms = part.at[g, core, colour]
            for s, way in ((0, 1), (1, -1)):
                beside, target = at_line(colour, way)
                line_copy(g, colour, terms.at[beside], arrived.at[g, colour, s], arrived_recv, target).start()

    def send_on(g):
        for colour in range(2):
            terms = part.at[g, core, colour]
            whole = between.at[g, colour]
            line_copy(g, colour, whole, whole, between_recv, peer).wait_recv()
            for s, way in ((0, 1), (1, -1)):
                there, target = at_line(colour, 2 * way)
                terms[there] = terms[there] + between[g, colour, s, :2]
                terms[there, s] = terms[there, s] + between[g, colour, s, 2]
                line_copy(g, colour, terms.at[there], arrived.at[g, colour, 2 + s], arrived_recv, target).start()

    multiply0(EARLY, CHUNKS, True)
    for n in range(HALF):
        x2_copy(n).wait_recv()
    multiply2()
    spread(0)
    for n in range(EARLY):
        x1_copy(chunk(n)).wait_recv()
    multiply1(0, EARLY, False)
    spread(2)
    for n in range(EARLY, CHUNKS):
        x1_copy(chunk(n)).wait_recv()
    multiply1(EARLY, CHUNKS, True)
    spread(1)
    send_on(0)
    send_on(2)
    send_on(1)
    pl.semaphore_wait(all_sem, 3)

    def cross_copy(b, colour, d):
        if colour == 0:
            here, there = y, (y + d) % 8
            target = device(x, there, z, core)
        else:
            here, there = z, (z + d) % 8
            target = device(x, y, there, core)
        groups = pl.ds(2 * b, len(BATCHES[b]))
        return copy_to(
            total.at[colour, there, groups], crossed.at[colour, here, groups],
            cross_send.at[b, colour], cross_recv.at[b, colour], target,
        )

    for n in range(CHUNKS):
        if n + AHEAD >= CHUNKS:
            for d in (1, 2, 3):
                y_copy(chunk(n), other_y(d)).wait_send()
        x1_copy(n).wait_send()
        if n < HALF:
            pass_copy(n).wait_send()
            x2_copy(n).wait_send()
    for g in range(3):
        for colour in range(2):
            core_copy(g, colour).wait_send()

    for b, groups in enumerate(BATCHES):
        for colour in range(2):
            for j, g in enumerate(groups):
                whole = arrived.at[g, colour]
                line_copy(g, colour, whole, whole, arrived_recv, peer).wait_recv()
                acc = part[g, core, colour, place(colour)]
                for d in range(4):
                    acc = acc + arrived[g, colour, d]
                total[colour, :, 2 * b + j] = acc.reshape(8, 8, 128)

            @pl.loop(1, 8)
            def _(d):
                cross_copy(b, colour, d).start()

    def tile_copies(colour, b, j, act):
        g = BATCHES[b][j]
        where, index = (z, y) if colour == 0 else (y, z)
        row = x * 4 + where // 2
        column = ((x + g) % 4) * 4 + 2 * colour + index // 4
        targets = [(1, column, 2 * row + where % 2, mirror.at[core, index % 4])]
        if g > 0:
            for k in range(2):
                targets.append((0, row, 2 * column + k, plain.at[where % 2, core, index % 4]))
        for kind, to_grp, to_cell, dst in targets:
            here = jnp.logical_and(to_grp == grp, to_cell == cell)
            act(piece.at[colour, 2 * b + j], dst, kind, here, (to_grp, to_cell))

    def start_tile(src, dst, kind, here, target):
        @pl.when(here)
        def _():
            pltpu.make_async_copy(src, dst, tile_recv.at[kind]).start()

        @pl.when(jnp.logical_not(here))
        def _():
            copy_to(src, dst, tile_send, tile_recv.at[kind], target).start()

    def finish_tile(src, dst, kind, here, target):
        @pl.when(jnp.logical_not(here))
        def _():
            copy_to(src, dst, tile_send, tile_recv.at[kind], target).wait_send()

    for b, groups in enumerate(BATCHES):
        for colour in range(2):
            here = y if colour == 0 else z
            slots = pl.ds(2 * b, len(groups))
            seven = crossed.at[colour, pl.ds(0, 7), slots]
            copy_to(seven, seven, cross_send.at[b, colour], cross_recv.at[b, colour], peer).wait_recv()
            acc = total[colour, here, slots]
            for d in range(1, 8):
                acc = acc + crossed[colour, (here + d) % 8, slots]
            piece[colour, slots] = acc
            for j in range(len(groups)):
                tile_copies(colour, b, j, start_tile)

    for g in range(3):
        for colour in range(2):
            seven = part.at[g, core, colour, pl.ds(0, 7)]
            line_copy(g, colour, seven, seven, arrived_recv, peer).wait_send()
    for b, groups in enumerate(BATCHES):
        for colour in range(2):
            seven = crossed.at[colour, pl.ds(0, 7), pl.ds(2 * b, len(groups))]
            copy_to(seven, seven, cross_send.at[b, colour], cross_recv.at[b, colour], peer).wait_send()
            for j in range(len(groups)):
                tile_copies(colour, b, j, finish_tile)

    apart = (cell // 8 - x) % 4
    has_plain = jnp.logical_or(apart == 1, apart == 2)

    @pl.when(jnp.logical_not(has_plain))
    def _():
        plain[...] = jnp.zeros_like(plain)

    @pl.when(apart == 1)
    def _():
        mirror[...] = jnp.zeros_like(mirror)

    @pl.when(has_plain)
    def _():
        copy_to(plain, plain, tile_send, tile_recv.at[0], peer).wait_recv()

    @pl.when(apart != 1)
    def _():
        copy_to(mirror, mirror, tile_send, tile_recv.at[1], peer).wait_recv()

    turned_back = plain[...].reshape(128, 128).T
    columns = jnp.where(core == 0, turned_back[:64], turned_back[64:])
    out_ref[...] = columns + mirror[...].reshape(64, 128)


def body(snapshots, density):
    f32, bf16, dma = jnp.float32, jnp.bfloat16, pltpu.SemaphoreType.DMA
    return pl.pallas_call(
        kernel,
        out_shape=jax.ShapeDtypeStruct((64, 128), f32),
        in_specs=[pl.BlockSpec(memory_space=pl.ANY), pl.BlockSpec(memory_space=pltpu.SMEM)],
        out_specs=pl.BlockSpec(memory_space=pltpu.VMEM),
        scratch_shapes=[
            pltpu.VMEM((SLAB, SNAP), bf16),
            pltpu.VMEM((4, CHUNKS, SNAP, WIDE), bf16),
            pltpu.VMEM((CHUNKS, 4, SNAP, WIDE), bf16),
            pltpu.VMEM((CHUNKS, 4, SNAP, WIDE), bf16),
            pltpu.VMEM((HALF, 4, SNAP, WIDE), bf16),
            pltpu.VMEM((HALF, 4, SNAP, WIDE), bf16),
            pltpu.VMEM((3, 2, 2, 8, 2, 32, 128), f32),
            pltpu.VMEM((3, 2, 8, 2, 32, 128), f32),
            pltpu.VMEM((3, 2, 2, 3, 32, 128), f32),
            pltpu.VMEM((3, 2, 4, 2, 32, 128), f32),
            pltpu.VMEM((2, 8, 3, 8, 128), f32),
            pltpu.VMEM((2, 8, 3, 8, 128), f32),
            pltpu.VMEM((2, 3, 8, 128), f32),
            pltpu.VMEM((2, 2, 4, 8, 128), f32),
            pltpu.VMEM((2, 4, 8, 128), f32),
            dma, dma((CHUNKS, 4)), dma((CHUNKS, 4)), *[dma((CHUNKS,))] * 2, *[dma((HALF,))] * 4, dma((3, 2)), dma((3, 2)),
            dma((3, 2)), dma((3, 2)), dma((3, 2)), dma((2, 2)), dma((2, 2)), dma, dma((2,)),
            pltpu.SemaphoreType.REGULAR, pltpu.SemaphoreType.REGULAR,
        ],
        compiler_params=pltpu.CompilerParams(
            collective_id=0, has_side_effects=True, vmem_limit_bytes=55000 * 1024
        ),
        cost_estimate=pl.CostEstimate(flops=10**9, bytes_accessed=10**6, transcendentals=0),
    )(snapshots, density).T * (1.0 / CELLS)


def solution(mesh):
    in_specs = (P("cell", "grp"), P())
    return jax.shard_map(body, mesh=mesh, in_specs=in_specs, out_specs=P("grp", "cell"), check_vma=False)
```

```python
import jax
import jax.numpy as jnp
from jax import lax
from jax.experimental import pallas as pl
from jax.experimental.pallas import tpu as pltpu
from jax.sharding import PartitionSpec as P

MESH = pl.DeviceIdType.MESH
CELLS = 98304
SLAB = 3072
QUARTER = SLAB // 4
CHUNKS = 6
HALF = CHUNKS // 2
AHEAD = 2
EARLY = 4
PIECED = 4
BATCHES = ((0, 2), (1,))
WIDE = QUARTER // CHUNKS
SNAP = 128


def device(x, y, z, core):
    return x * 4 + y % 4, (z * 2 + y // 4) * 2 + core


def copy_to(src, dst, send, recv, target):
    return pltpu.make_async_remote_copy(
        src_ref=src, dst_ref=dst, send_sem=send, recv_sem=recv, device_id=target, device_id_type=MESH
    )


def kernel(
    snap_hbm, density_ref, out_ref,
    snap, turned, own, next1, passing, next2, part, peer_part, between, arrived, total, crossed, piece, plain, mirror,
    load_sem, y_send, y_recv, x1_send, x1_recv, pass_send, pass_recv, x2_send, x2_recv, core_send, core_recv,
    line_send, between_recv, arrived_recv, cross_send, cross_recv, tile_send, tile_recv, plane_sem, all_sem,
):
    grp, cell = lax.axis_index("grp"), lax.axis_index("cell")
    x, ylo, z, core = grp // 4, grp % 4, cell // 4, cell % 2
    y = (cell // 2) % 2 * 4 + ylo
    y_base = y - ylo
    peer = (grp, cell + 1 - 2 * core)

    half = x // 2
    first_chunk = (1 - half) * HALF

    def chunk(n):
        return (n + first_chunk) % CHUNKS

    def load(c):
        return pltpu.make_async_copy(snap_hbm.at[:, c], snap.at[:, c], load_sem.at[c])

    for n in range(CHUNKS):
        load(chunk(n)).start()

    barrier = pltpu.get_barrier_semaphore()

    def greet(sem, d, axis):
        target = {
            "x": lambda: device((x + d) % 4, y, z, core),
            "y": lambda: device(x, (y + d) % 8, z, core),
            "z": lambda: device(x, y, (z + d) % 8, core),
        }[axis]()
        pl.semaphore_signal(sem, inc=1, device_id=target, device_id_type=MESH)

    for d in range(1, 4):
        greet(barrier, d, "x")
    for d in range(1, 8):
        greet(barrier, d, "y")
        greet(barrier, d, "z")
    pl.semaphore_signal(barrier, inc=1, device_id=peer, device_id_type=MESH)

    scale = jnp.sqrt(jnp.full((1, SNAP), density_ref[z], jnp.float32))

    def weigh(c):
        load(c).wait()
        for q in range(4):
            turned[q, c] = (snap[q, c].astype(jnp.float32) * scale).astype(jnp.bfloat16).T
        own[c, ylo] = turned[ylo, c]

    def other_y(d):
        return (ylo + d) % 4

    def y_copy(c, q):
        return copy_to(
            turned.at[q, c], own.at[c, ylo], y_send.at[c, q], y_recv.at[c, ylo], device(x, y_base + q, z, core)
        )

    def y_arrival(c, q):
        return copy_to(
            turned.at[q, c], own.at[c, q], y_send.at[c, q], y_recv.at[c, q], device(x, y_base + q, z, core)
        )

    def x1_copy(c):
        return copy_to(own.at[c], next1.at[c], x1_send.at[c], x1_recv.at[c], device((x + 3) % 4, y, z, core))

    def x1_piece(c, q):
        return copy_to(
            own.at[c, q], next1.at[c, q], x1_send.at[c], x1_recv.at[c], device((x + 3) % 4, y, z, core)
        )

    def pass_copy(n):
        return copy_to(
            own.at[chunk(n)], passing.at[n], pass_send.at[n], pass_recv.at[n], device((x + 1) % 4, y, z, core)
        )

    def x2_copy(n):
        return copy_to(
            passing.at[n], next2.at[n], x2_send.at[n], x2_recv.at[n], device((x + 1) % 4, y, z, core)
        )

    def start_y(n):
        for d in (1, 2, 3):
            y_copy(chunk(n), other_y(d)).start()

    weigh(chunk(0))
    pl.semaphore_wait(barrier, 18)
    for n in range(CHUNKS):
        if n > 0:
            weigh(chunk(n))
        if n < AHEAD:
            start_y(n)
        if n >= PIECED:
            x1_piece(chunk(n), ylo).start()

    for d in range(1, 8):
        greet(plane_sem, d, "y")

    def multiply(g, colour, pairs, more=False):
        left = jnp.concatenate([pair[0] for pair in pairs], axis=-1).reshape(512, len(pairs) * WIDE)
        right = jnp.concatenate([pair[1] for pair in pairs], axis=-1).reshape(256, len(pairs) * WIDE)
        product = lax.dot_general(left, right, (((1,), (1,)), ((), ())), preferred_element_type=jnp.float32)
        for n in range(8):
            for h in range(2):
                for t in range(2):
                    term = product[n * 64 + h * 32 : n * 64 + h * 32 + 32, t * 128 : t * 128 + 128]
                    if more:
                        term = term + part[g, h, colour, n, t]
                    part[g, h, colour, n, t] = term

    def core_copy(g, colour):
        return copy_to(
            part.at[g, 1 - core, colour], peer_part.at[g, colour],
            core_send.at[g, colour], core_recv.at[g, colour], peer,
        )

    def columns_of(colour):
        return slice(2 * colour, 2 * colour + 2)

    def multiply0(first, last, more):
        for colour in range(2):
            multiply(
                0, colour, [(own[chunk(n)], own[chunk(n), columns_of(colour)]) for n in range(first, last)], more
            )
            if more:
                core_copy(0, colour).start()

    def multiply1(first, last, more):
        for colour in range(2):
            multiply(
                1, colour, [(own[chunk(n)], next1[chunk(n), columns_of(colour)]) for n in range(first, last)], more
            )
            if more:
                core_copy(1, colour).start()

    def multiply2():
        for colour in range(2):
            multiply(2, colour, [(own[half * HALF + n], next2[n, columns_of(colour)]) for n in range(HALF)])
            core_copy(2, colour).start()

    for n in range(CHUNKS):
        for d in (1, 2, 3):
            y_arrival(chunk(n), other_y(d)).wait_recv()
            if n >= PIECED:
                x1_piece(chunk(n), other_y(d)).start()
        if n + AHEAD < CHUNKS:
            for d in (1, 2, 3):
                y_copy(chunk(n), other_y(d)).wait_send()
            start_y(n + AHEAD)
        if n < PIECED:
            x1_copy(chunk(n)).start()
        if n < HALF:
            pass_copy(n).start()
        if 2 <= n < HALF + 2:
            pass_copy(n - 2).wait_recv()
            x2_copy(n - 2).start()
        if n == EARLY:
            multiply0(0, EARLY, False)

    pl.semaphore_wait(plane_sem, 7)
    for d in range(1, 4):
        greet(all_sem, d, "x")

    def place(colour):
        return z if colour == 0 else y

    def at_line(colour, d):
        there = (place(colour) + d + 8) % 8
        return there, device(x, y, there, core) if colour == 0 else device(x, there, z, core)

    def line_copy(g, colour, src, dst, recv, target):
        return copy_to(src, dst, line_send.at[g, colour], recv.at[g, colour], target)

    def spread(g):
        for colour in range(2):
            core_copy(g, colour).wait_recv()
            part[g, core, colour] = part[g, core, colour] + peer_part[g, colour]
            terms = part.at[g, core, colour]
            for s, way in ((0, 1), (1, -1)):
                third, _ = at_line(colour, 3 * way)
                fourth, _ = at_line(colour, 4)
                _, target = at_line(colour, way)
                _, target2 = at_line(colour, 2 * way)
                slot = between.at[g, colour, s]
                line_copy(g, colour, terms.at[third], slot.at[pl.ds(0, 2)], between_recv, target).start()
                line_copy(g, colour, terms.at[fourth, s], slot.at[2], between_recv, target2).start()
        for colour in range(2):
            terms = part.at[g, core, colour]
            for s, way in ((0, 1), (1, -1)):
                beside, target = at_line(colour, way)
                line_copy(g, colour, terms.at[beside], arrived.at[g, colour, s], arrived_recv, target).start()

    def send_on(g):
        for colour in range(2):
            terms = part.at[g, core, colour]
            whole = between.at[g, colour]
            line_copy(g, colour, whole, whole, between_recv, peer).wait_recv()
            for s, way in ((0, 1), (1, -1)):
                there, target = at_line(colour, 2 * way)
                terms[there] = terms[there] + between[g, colour, s, :2]
                terms[there, s] = terms[there, s] + between[g, colour, s, 2]
                line_copy(g, colour, terms.at[there], arrived.at[g, colour, 2 + s], arrived_recv, target).start()

    multiply0(EARLY, CHUNKS, True)
    for n in range(HALF):
        x2_copy(n).wait_recv()
    multiply2()
    spread(0)
    for n in range(EARLY):
        x1_copy(chunk(n)).wait_recv()
    multiply1(0, EARLY, False)
    spread(2)
    for n in range(EARLY, CHUNKS):
        x1_copy(chunk(n)).wait_recv()
    multiply1(EARLY, CHUNKS, True)
    spread(1)
    send_on(0)
    send_on(2)
    send_on(1)
    pl.semaphore_wait(all_sem, 3)

    def cross_copy(b, colour, d):
        if colour == 0:
            here, there = y, (y + d) % 8
            target = device(x, there, z, core)
        else:
            here, there = z, (z + d) % 8
            target = device(x, y, there, core)
        groups = pl.ds(2 * b, len(BATCHES[b]))
        return copy_to(
            total.at[colour, there, groups], crossed.at[colour, here, groups],
            cross_send.at[b, colour], cross_recv.at[b, colour], target,
        )

    for n in range(CHUNKS):
        if n + AHEAD >= CHUNKS:
            for d in (1, 2, 3):
                y_copy(chunk(n), other_y(d)).wait_send()
        x1_copy(n).wait_send()
        if n < HALF:
            pass_copy(n).wait_send()
            x2_copy(n).wait_send()
    for g in range(3):
        for colour in range(2):
            core_copy(g, colour).wait_send()

    for b, groups in enumerate(BATCHES):
        for colour in range(2):
            for j, g in enumerate(groups):
                whole = arrived.at[g, colour]
                line_copy(g, colour, whole, whole, arrived_recv, peer).wait_recv()
                acc = part[g, core, colour, place(colour)]
                for d in range(4):
                    acc = acc + arrived[g, colour, d]
                total[colour, :, 2 * b + j] = acc.reshape(8, 8, 128)

            @pl.loop(1, 8)
            def _(d):
                cross_copy(b, colour, d).start()

    def tile_copies(colour, b, j, act):
        g = BATCHES[b][j]
        where, index = (z, y) if colour == 0 else (y, z)
        row = x * 4 + where // 2
        column = ((x + g) % 4) * 4 + 2 * colour + index // 4
        targets = [(1, column, 2 * row + where % 2, mirror.at[core, index % 4])]
        if g > 0:
            for k in range(2):
                targets.append((0, row, 2 * column + k, plain.at[where % 2, core, index % 4]))
        for kind, to_grp, to_cell, dst in targets:
            here = jnp.logical_and(to_grp == grp, to_cell == cell)
            act(piece.at[colour, 2 * b + j], dst, kind, here, (to_grp, to_cell))

    def start_tile(src, dst, kind, here, target):
        @pl.when(here)
        def _():
            pltpu.make_async_copy(src, dst, tile_recv.at[kind]).start()

        @pl.when(jnp.logical_not(here))
        def _():
            copy_to(src, dst, tile_send, tile_recv.at[kind], target).start()

    def finish_tile(src, dst, kind, here, target):
        @pl.when(jnp.logical_not(here))
        def _():
            copy_to(src, dst, tile_send, tile_recv.at[kind], target).wait_send()

    for b, groups in enumerate(BATCHES):
        for colour in range(2):
            here = y if colour == 0 else z
            slots = pl.ds(2 * b, len(groups))
            seven = crossed.at[colour, pl.ds(0, 7), slots]
            copy_to(seven, seven, cross_send.at[b, colour], cross_recv.at[b, colour], peer).wait_recv()
            acc = total[colour, here, slots]
            for d in range(1, 8):
                acc = acc + crossed[colour, (here + d) % 8, slots]
            piece[colour, slots] = acc
            for j in range(len(groups)):
                tile_copies(colour, b, j, start_tile)

    for g in range(3):
        for colour in range(2):
            seven = part.at[g, core, colour, pl.ds(0, 7)]
            line_copy(g, colour, seven, seven, arrived_recv, peer).wait_send()
    for b, groups in enumerate(BATCHES):
        for colour in range(2):
            seven = crossed.at[colour, pl.ds(0, 7), pl.ds(2 * b, len(groups))]
            copy_to(seven, seven, cross_send.at[b, colour], cross_recv.at[b, colour], peer).wait_send()
            for j in range(len(groups)):
                tile_copies(colour, b, j, finish_tile)

    apart = (cell // 8 - x) % 4
    has_plain = jnp.logical_or(apart == 1, apart == 2)

    @pl.when(jnp.logical_not(has_plain))
    def _():
        plain[...] = jnp.zeros_like(plain)

    @pl.when(apart == 1)
    def _():
        mirror[...] = jnp.zeros_like(mirror)

    @pl.when(has_plain)
    def _():
        copy_to(plain, plain, tile_send, tile_recv.at[0], peer).wait_recv()

    @pl.when(apart != 1)
    def _():
        copy_to(mirror, mirror, tile_send, tile_recv.at[1], peer).wait_recv()

    turned_back = plain[...].reshape(128, 128).T
    columns = jnp.where(core == 0, turned_back[:64], turned_back[64:])
    out_ref[...] = columns + mirror[...].reshape(64, 128)


def body(snapshots, density):
    f32, bf16, dma = jnp.float32, jnp.bfloat16, pltpu.SemaphoreType.DMA
    return pl.pallas_call(
        kernel,
        out_shape=jax.ShapeDtypeStruct((64, 128), f32),
        in_specs=[pl.BlockSpec(memory_space=pl.ANY), pl.BlockSpec(memory_space=pltpu.SMEM)],
        out_specs=pl.BlockSpec(memory_space=pltpu.VMEM),
        scratch_shapes=[
            pltpu.VMEM((4, CHUNKS, WIDE, SNAP), bf16),
            pltpu.VMEM((4, CHUNKS, SNAP, WIDE), bf16),
            pltpu.VMEM((CHUNKS, 4, SNAP, WIDE), bf16),
            pltpu.VMEM((CHUNKS, 4, SNAP, WIDE), bf16),
            pltpu.VMEM((HALF, 4, SNAP, WIDE), bf16),
            pltpu.VMEM((HALF, 4, SNAP, WIDE), bf16),
            pltpu.VMEM((3, 2, 2, 8, 2, 32, 128), f32),
            pltpu.VMEM((3, 2, 8, 2, 32, 128), f32),
            pltpu.VMEM((3, 2, 2, 3, 32, 128), f32),
            pltpu.VMEM((3, 2, 4, 2, 32, 128), f32),
            pltpu.VMEM((2, 8, 3, 8, 128), f32),
            pltpu.VMEM((2, 8, 3, 8, 128), f32),
            pltpu.VMEM((2, 3, 8, 128), f32),
            pltpu.VMEM((2, 2, 4, 8, 128), f32),
            pltpu.VMEM((2, 4, 8, 128), f32),
            dma((CHUNKS,)), dma((CHUNKS, 4)), dma((CHUNKS, 4)), *[dma((CHUNKS,))] * 2, *[dma((HALF,))] * 4, dma((3, 2)), dma((3, 2)),
            dma((3, 2)), dma((3, 2)), dma((3, 2)), dma((2, 2)), dma((2, 2)), dma, dma((2,)),
            pltpu.SemaphoreType.REGULAR, pltpu.SemaphoreType.REGULAR,
        ],
        compiler_params=pltpu.CompilerParams(
            collective_id=0, has_side_effects=True, vmem_limit_bytes=55000 * 1024
        ),
        cost_estimate=pl.CostEstimate(flops=10**9, bytes_accessed=10**6, transcendentals=0),
    )(snapshots.reshape(4, CHUNKS, WIDE, SNAP), density).T * (1.0 / CELLS)


def solution(mesh):
    in_specs = (P("cell", "grp"), P())
    return jax.shard_map(body, mesh=mesh, in_specs=in_specs, out_specs=P("grp", "cell"), check_vma=False)
```

```python
import jax
import jax.numpy as jnp
from jax import lax
from jax.experimental import pallas as pl
from jax.experimental.pallas import tpu as pltpu
from jax.sharding import PartitionSpec as P

MESH = pl.DeviceIdType.MESH
CELLS = 98304
SLAB = 3072
QUARTER = SLAB // 4
CHUNKS = 6
HALF = CHUNKS // 2
AHEAD = 2
EARLY = 4
PIECED = 4
BATCHES = ((0, 2), (1,))
WIDE = QUARTER // CHUNKS
SNAP = 128


def device(x, y, z, core):
    return x * 4 + y % 4, (z * 2 + y // 4) * 2 + core


def copy_to(src, dst, send, recv, target):
    return pltpu.make_async_remote_copy(
        src_ref=src, dst_ref=dst, send_sem=send, recv_sem=recv, device_id=target, device_id_type=MESH
    )


def kernel(
    snap_hbm, density_ref, out_ref,
    snap, turned, own, next1, passing, next2, part, peer_part, between, arrived, total, crossed, piece, plain, mirror,
    load_sem, y_send, y_recv, x1_send, x1_recv, pass_send, pass_recv, x2_send, x2_recv, core_send, core_recv,
    line_send, between_recv, arrived_recv, cross_send, cross_recv, tile_send, tile_recv, plane_sem, all_sem,
):
    grp, cell = lax.axis_index("grp"), lax.axis_index("cell")
    x, ylo, z, core = grp // 4, grp % 4, cell // 4, cell % 2
    y = (cell // 2) % 2 * 4 + ylo
    y_base = y - ylo
    peer = (grp, cell + 1 - 2 * core)

    load = pltpu.make_async_copy(snap_hbm, snap, load_sem)
    load.start()

    barrier = pltpu.get_barrier_semaphore()

    def greet(sem, d, axis):
        target = {
            "x": lambda: device((x + d) % 4, y, z, core),
            "y": lambda: device(x, (y + d) % 8, z, core),
            "z": lambda: device(x, y, (z + d) % 8, core),
        }[axis]()
        pl.semaphore_signal(sem, inc=1, device_id=target, device_id_type=MESH)

    for d in range(1, 4):
        greet(barrier, d, "x")
    for d in range(1, 8):
        greet(barrier, d, "y")
        greet(barrier, d, "z")
    pl.semaphore_signal(barrier, inc=1, device_id=peer, device_id_type=MESH)

    half = x // 2
    first_chunk = (1 - half) * HALF

    def chunk(n):
        return (n + first_chunk) % CHUNKS

    load.wait()
    scale = jnp.sqrt(jnp.full((1, SNAP), density_ref[z], jnp.float32))

    def weigh(c):
        for q in range(4):
            rows = pl.ds(pl.multiple_of(q * QUARTER + c * WIDE, WIDE), WIDE)
            turned[q, c] = (snap[rows, :].astype(jnp.float32) * scale).astype(jnp.bfloat16).T
        own[c, ylo] = turned[ylo, c]

    def other_y(d):
        return (ylo + d) % 4

    def y_copy(c, q):
        return copy_to(
            turned.at[q, c], own.at[c, ylo], y_send.at[c, q], y_recv.at[c, ylo], device(x, y_base + q, z, core)
        )

    def y_arrival(c, q):
        return copy_to(
            turned.at[q, c], own.at[c, q], y_send.at[c, q], y_recv.at[c, q], device(x, y_base + q, z, core)
        )

    def x1_copy(c):
        return copy_to(own.at[c], next1.at[c], x1_send.at[c], x1_recv.at[c], device((x + 3) % 4, y, z, core))

    def x1_piece(c, q):
        return copy_to(
            own.at[c, q], next1.at[c, q], x1_send.at[c], x1_recv.at[c], device((x + 3) % 4, y, z, core)
        )

    def pass_copy(n):
        return copy_to(
            own.at[chunk(n)], passing.at[n], pass_send.at[n], pass_recv.at[n], device((x + 1) % 4, y, z, core)
        )

    def x2_copy(n):
        return copy_to(
            passing.at[n], next2.at[n], x2_send.at[n], x2_recv.at[n], device((x + 1) % 4, y, z, core)
        )

    def start_y(n):
        for d in (1, 2, 3):
            y_copy(chunk(n), other_y(d)).start()

    weigh(chunk(0))
    pl.semaphore_wait(barrier, 18)
    for n in range(CHUNKS):
        if n > 0:
            weigh(chunk(n))
        if n < AHEAD:
            start_y(n)
        if n >= PIECED:
            x1_piece(chunk(n), ylo).start()

    for d in range(1, 8):
        greet(plane_sem, d, "y")

    def multiply(g, colour, pairs, more=False):
        left = jnp.concatenate([pair[0] for pair in pairs], axis=-1).reshape(512, len(pairs) * WIDE)
        right = jnp.concatenate([pair[1] for pair in pairs], axis=-1).reshape(256, len(pairs) * WIDE)
        product = lax.dot_general(left, right, (((1,), (1,)), ((), ())), preferred_element_type=jnp.float32)
        for n in range(8):
            for h in range(2):
                for t in range(2):
                    term = product[n * 64 + h * 32 : n * 64 + h * 32 + 32, t * 128 : t * 128 + 128]
                    if more:
                        term = term + part[g, h, colour, n, t]
                    part[g, h, colour, n, t] = term

    def core_copy(g, colour):
        return copy_to(
            part.at[g, 1 - core, colour], peer_part.at[g, colour],
            core_send.at[g, colour], core_recv.at[g, colour], peer,
        )

    def columns_of(colour):
        return slice(2 * colour, 2 * colour + 2)

    def multiply0(first, last, more):
        for colour in range(2):
            multiply(
                0, colour, [(own[chunk(n)], own[chunk(n), columns_of(colour)]) for n in range(first, last)], more
            )
            if more:
                core_copy(0, colour).start()

    def multiply1(first, last, more):
        for colour in range(2):
            multiply(
                1, colour, [(own[chunk(n)], next1[chunk(n), columns_of(colour)]) for n in range(first, last)], more
            )
            if more:
                core_copy(1, colour).start()

    def multiply2():
        for colour in range(2):
            multiply(2, colour, [(own[half * HALF + n], next2[n, columns_of(colour)]) for n in range(HALF)])
            core_copy(2, colour).start()

    for n in range(CHUNKS):
        for d in (1, 2, 3):
            y_arrival(chunk(n), other_y(d)).wait_recv()
            if n >= PIECED:
                x1_piece(chunk(n), other_y(d)).start()
        if n + AHEAD < CHUNKS:
            for d in (1, 2, 3):
                y_copy(chunk(n), other_y(d)).wait_send()
            start_y(n + AHEAD)
        if n < PIECED:
            x1_copy(chunk(n)).start()
        if n < HALF:
            pass_copy(n).start()
        if 2 <= n < HALF + 2:
            pass_copy(n - 2).wait_recv()
            x2_copy(n - 2).start()
        if n == EARLY:
            multiply0(0, EARLY, False)

    pl.semaphore_wait(plane_sem, 7)
    for d in range(1, 4):
        greet(all_sem, d, "x")

    def place(colour):
        return z if colour == 0 else y

    line_shift = (2 * x + 5, 5)
    rows_here = ((z + 16 - line_shift[0]) % 8, (y + 16 - line_shift[1]) % 8)
    cross_shift = (4 * (rows_here[0] // 2) + 5, 7 * (rows_here[1] // 2) + 2 * x + 7)

    def part_of(colour, there):
        return (there + 40 - cross_shift[colour]) % 8

    def at_line(colour, d):
        there = (place(colour) + d + 8) % 8
        rows = (there + 16 - line_shift[colour]) % 8
        return rows, device(x, y, there, core) if colour == 0 else device(x, there, z, core)

    def line_copy(g, colour, src, dst, recv, target):
        return copy_to(src, dst, line_send.at[g, colour], recv.at[g, colour], target)

    def spread(g):
        for colour in range(2):
            core_copy(g, colour).wait_recv()
            part[g, core, colour] = part[g, core, colour] + peer_part[g, colour]
            terms = part.at[g, core, colour]
            for s, way in ((0, 1), (1, -1)):
                third, _ = at_line(colour, 3 * way)
                fourth, _ = at_line(colour, 4)
                _, target = at_line(colour, way)
                _, target2 = at_line(colour, 2 * way)
                slot = between.at[g, colour, s]
                line_copy(g, colour, terms.at[third], slot.at[pl.ds(0, 2)], between_recv, target).start()
                line_copy(g, colour, terms.at[fourth, s], slot.at[2], between_recv, target2).start()
        for colour in range(2):
            terms = part.at[g, core, colour]
            for s, way in ((0, 1), (1, -1)):
                beside, target = at_line(colour, way)
                line_copy(g, colour, terms.at[beside], arrived.at[g, colour, s], arrived_recv, target).start()

    def send_on(g):
        for colour in range(2):
            terms = part.at[g, core, colour]
            whole = between.at[g, colour]
            line_copy(g, colour, whole, whole, between_recv, peer).wait_recv()
            for s, way in ((0, 1), (1, -1)):
                there, target = at_line(colour, 2 * way)
                terms[there] = terms[there] + between[g, colour, s, :2]
                terms[there, s] = terms[there, s] + between[g, colour, s, 2]
                line_copy(g, colour, terms.at[there], arrived.at[g, colour, 2 + s], arrived_recv, target).start()

    multiply0(EARLY, CHUNKS, True)
    for n in range(HALF):
        x2_copy(n).wait_recv()
    multiply2()
    spread(0)
    for n in range(EARLY):
        x1_copy(chunk(n)).wait_recv()
    multiply1(0, EARLY, False)
    spread(2)
    for n in range(EARLY, CHUNKS):
        x1_copy(chunk(n)).wait_recv()
    multiply1(EARLY, CHUNKS, True)
    spread(1)
    send_on(0)
    send_on(2)
    send_on(1)
    pl.semaphore_wait(all_sem, 3)

    def cross_copy(b, colour, d):
        if colour == 0:
            here, there = y, (y + d) % 8
            target = device(x, there, z, core)
        else:
            here, there = z, (z + d) % 8
            target = device(x, y, there, core)
        groups = pl.ds(2 * b, len(BATCHES[b]))
        return copy_to(
            total.at[colour, part_of(colour, there), groups], crossed.at[colour, here, groups],
            cross_send.at[b, colour], cross_recv.at[b, colour], target,
        )

    for n in range(CHUNKS):
        if n + AHEAD >= CHUNKS:
            for d in (1, 2, 3):
                y_copy(chunk(n), other_y(d)).wait_send()
        x1_copy(n).wait_send()
        if n < HALF:
            pass_copy(n).wait_send()
            x2_copy(n).wait_send()
    for g in range(3):
        for colour in range(2):
            core_copy(g, colour).wait_send()

    for b, groups in enumerate(BATCHES):
        for colour in range(2):
            for j, g in enumerate(groups):
                whole = arrived.at[g, colour]
                line_copy(g, colour, whole, whole, arrived_recv, peer).wait_recv()
                acc = part[g, core, colour, rows_here[colour]]
                for d in range(4):
                    acc = acc + arrived[g, colour, d]
                total[colour, :, 2 * b + j] = acc.reshape(8, 8, 128)

            @pl.loop(1, 8)
            def _(d):
                cross_copy(b, colour, d).start()

    def tile_copies(colour, b, j, act):
        g = BATCHES[b][j]
        where, index = rows_here[colour], part_of(colour, y if colour == 0 else z)
        row = x * 4 + where // 2
        column = ((x + g) % 4) * 4 + 2 * colour + index // 4
        targets = [(1, column, 2 * row + where % 2, mirror.at[core, index % 4])]
        if g > 0:
            for k in range(2):
                targets.append((0, row, 2 * column + k, plain.at[where % 2, core, index % 4]))
        for kind, to_grp, to_cell, dst in targets:
            here = jnp.logical_and(to_grp == grp, to_cell == cell)
            act(piece.at[colour, 2 * b + j], dst, kind, here, (to_grp, to_cell))

    def start_tile(src, dst, kind, here, target):
        @pl.when(here)
        def _():
            pltpu.make_async_copy(src, dst, tile_recv.at[kind]).start()

        @pl.when(jnp.logical_not(here))
        def _():
            copy_to(src, dst, tile_send, tile_recv.at[kind], target).start()

    def finish_tile(src, dst, kind, here, target):
        @pl.when(jnp.logical_not(here))
        def _():
            copy_to(src, dst, tile_send, tile_recv.at[kind], target).wait_send()

    for b, groups in enumerate(BATCHES):
        for colour in range(2):
            here = y if colour == 0 else z
            slots = pl.ds(2 * b, len(groups))
            seven = crossed.at[colour, pl.ds(0, 7), slots]
            copy_to(seven, seven, cross_send.at[b, colour], cross_recv.at[b, colour], peer).wait_recv()
            acc = total[colour, part_of(colour, here), slots]
            for d in range(1, 8):
                acc = acc + crossed[colour, (here + d) % 8, slots]
            piece[colour, slots] = acc
            for j in range(len(groups)):
                tile_copies(colour, b, j, start_tile)

    for g in range(3):
        for colour in range(2):
            seven = part.at[g, core, colour, pl.ds(0, 7)]
            line_copy(g, colour, seven, seven, arrived_recv, peer).wait_send()
    for b, groups in enumerate(BATCHES):
        for colour in range(2):
            seven = crossed.at[colour, pl.ds(0, 7), pl.ds(2 * b, len(groups))]
            copy_to(seven, seven, cross_send.at[b, colour], cross_recv.at[b, colour], peer).wait_send()
            for j in range(len(groups)):
                tile_copies(colour, b, j, finish_tile)

    apart = (cell // 8 - x) % 4
    has_plain = jnp.logical_or(apart == 1, apart == 2)

    @pl.when(jnp.logical_not(has_plain))
    def _():
        plain[...] = jnp.zeros_like(plain)

    @pl.when(apart == 1)
    def _():
        mirror[...] = jnp.zeros_like(mirror)

    @pl.when(has_plain)
    def _():
        copy_to(plain, plain, tile_send, tile_recv.at[0], peer).wait_recv()

    @pl.when(apart != 1)
    def _():
        copy_to(mirror, mirror, tile_send, tile_recv.at[1], peer).wait_recv()

    turned_back = plain[...].reshape(128, 128).T
    columns = jnp.where(core == 0, turned_back[:64], turned_back[64:])
    out_ref[...] = columns + mirror[...].reshape(64, 128)


def body(snapshots, density):
    f32, bf16, dma = jnp.float32, jnp.bfloat16, pltpu.SemaphoreType.DMA
    return pl.pallas_call(
        kernel,
        out_shape=jax.ShapeDtypeStruct((64, 128), f32),
        in_specs=[pl.BlockSpec(memory_space=pl.ANY), pl.BlockSpec(memory_space=pltpu.SMEM)],
        out_specs=pl.BlockSpec(memory_space=pltpu.VMEM),
        scratch_shapes=[
            pltpu.VMEM((SLAB, SNAP), bf16),
            pltpu.VMEM((4, CHUNKS, SNAP, WIDE), bf16),
            pltpu.VMEM((CHUNKS, 4, SNAP, WIDE), bf16),
            pltpu.VMEM((CHUNKS, 4, SNAP, WIDE), bf16),
            pltpu.VMEM((HALF, 4, SNAP, WIDE), bf16),
            pltpu.VMEM((HALF, 4, SNAP, WIDE), bf16),
            pltpu.VMEM((3, 2, 2, 8, 2, 32, 128), f32),
            pltpu.VMEM((3, 2, 8, 2, 32, 128), f32),
            pltpu.VMEM((3, 2, 2, 3, 32, 128), f32),
            pltpu.VMEM((3, 2, 4, 2, 32, 128), f32),
            pltpu.VMEM((2, 8, 3, 8, 128), f32),
            pltpu.VMEM((2, 8, 3, 8, 128), f32),
            pltpu.VMEM((2, 3, 8, 128), f32),
            pltpu.VMEM((2, 2, 4, 8, 128), f32),
            pltpu.VMEM((2, 4, 8, 128), f32),
            dma, dma((CHUNKS, 4)), dma((CHUNKS, 4)), *[dma((CHUNKS,))] * 2, *[dma((HALF,))] * 4, dma((3, 2)), dma((3, 2)),
            dma((3, 2)), dma((3, 2)), dma((3, 2)), dma((2, 2)), dma((2, 2)), dma, dma((2,)),
            pltpu.SemaphoreType.REGULAR, pltpu.SemaphoreType.REGULAR,
        ],
        compiler_params=pltpu.CompilerParams(
            collective_id=0, has_side_effects=True, vmem_limit_bytes=55000 * 1024
        ),
        cost_estimate=pl.CostEstimate(flops=10**9, bytes_accessed=10**6, transcendentals=0),
    )(snapshots, density).T * (1.0 / CELLS)


def solution(mesh):
    in_specs = (P("cell", "grp"), P())
    return jax.shard_map(body, mesh=mesh, in_specs=in_specs, out_specs=P("grp", "cell"), check_vma=False)
```
